32 devices in a mesh: grp: 2 (over y), off: 4 (over x, core), tile: 4 (over z).
Axes of the slice: x: 2, y: 2, z: 4, core: 2. Of those that a mesh axis runs over, the one named last changes fastest.
Arguments:
- traces: bfloat16 [4096, 4096], P(('grp', 'off', 'tile')), parts along dimension 0, may hold values from -6 to 6
- class_map: int32 [4096, 1], P(('grp', 'off', 'tile')), parts along dimension 0, may hold values from 0 to 3; in each aligned block of 128 rows (0 to 127, 128 to 255, ...) at most 48 rows name the same one
- mid_bins: int32 [4096], P(('grp', 'off', 'tile')), parts along dimension 0, may hold values from 0 to 127
- fold_count: int32 [8], P(('grp', 'off')), parts along dimension 0, may hold values from 1 to 8
- weight_tiles: bfloat16 [4, 4, 128, 128], P('off'), may hold values from -0.09375 to 0.09375
- apertures: int32 [64, 32], P(('grp', 'off', 'tile')), parts along dimension 0, may hold values from 0 to 4
Outputs:
- image_tiles: float32 [64, 128, 128], P(('grp', 'off', 'tile')), parts along dimension 0
The draws below stay inside these ranges and needn't reach their ends.
There are 2 independent parts, one for each index of `grp`. The reference program is written for one: setup_inputs(seed, part) draws one part's arguments, and reference() takes and returns one part's arrays. A program takes and returns all parts, laid end to end along the dimension named above; an argument that names none is the same for every part. Nothing has to cross between parts.
Inputs may be any that keep to these rules, and one draw needn't show every extreme that they name: `class_map`: in the rows of one device each class is named by at most 48 traces; some class is named by exactly 48 traces on some device.
All inputs are finite; a program needn't handle non-finite values.
Results may differ from the reference program's by a relative error of at most 0.0025.
Values may be sent and summed in bfloat16 or wider, within the bound.
No kernel may reach another device: no remote copies, remote signals or barrier semaphores. Data moves between devices by JAX's collectives and lax.ppermute only.
A program may use at most 64 MiB of HBM per device.

```python
import math
import jax
import jax.numpy as jnp
import numpy as np
from jax import lax

TR_DEV = 128
BANDS = 32
BAND = 128
PTS = 128
MB = 128
TIL_DEV = 2
NPAT = 4
CLASSES = 4
CAP = 48
TRACES = 2048
TILES = 32
N_OFF = 4
N_TILE = 4


def with_ends(result, rng, least, largest):
    shape = result.shape
    index_at = [jax.random.randint(jax.random.fold_in(rng, axis), (), 0, shape[axis]) for axis in range(len(shape))]
    result = result.at[tuple(index_at)].set(least)
    longest = shape.index(max(shape))
    index_at[longest] = (index_at[longest] + 1) % shape[longest]
    return result.at[tuple(index_at)].set(largest)


def levels(own_key, shape, pieces, low, largest):
    def one(position, shards_of):
        steps = jax.random.uniform(jax.random.fold_in(jax.random.fold_in(own_key, 6), position), (shards_of,), jnp.float32, low / len(pieces), largest / len(pieces))
        return jnp.repeat(jnp.exp(steps), shape[position] // shards_of).reshape((-1,) + (1,) * (len(shape) - position - 1))

    loudness = one(*pieces[0])
    for cut in pieces[1:]:
        loudness = loudness * one(*cut)
    return loudness


def deal_out(key, own, number, rows, amount, top, reach, skew):
    sequence = jax.random.permutation(key, amount)
    heavy_load, usual = load_shares(amount, rows * top, reach, skew, True), load_shares(amount, rows * top, reach, skew, False)
    places = jnp.arange(amount)

    def named(lengths, rotation):
        used = int((lengths > 0).sum())
        fixed = max(1, used // 4)
        moved = fixed + (places - fixed + rotation * (used - fixed)) % max(1, amount - fixed)
        return jnp.zeros((amount,), jnp.int32).at[sequence[jnp.where(places < fixed, places, moved)]].set(jnp.asarray(lengths, jnp.int32))

    lengths = jnp.where(number % 4 == 0, named(heavy_load, number // 4), named(usual, number - number // 4 - 1))
    mixed = jax.random.permutation(jax.random.fold_in(own, 3), amount)
    giver, receiver = mixed[0:amount // 2 * 2:2], mixed[1:amount // 2 * 2:2]
    margin = jnp.minimum(lengths[giver] - 1, reach - lengths[receiver]) // 2
    margin = jnp.where((giver == sequence[0]) | (receiver == sequence[0]) | (lengths[receiver] == 0), 0, jnp.maximum(margin, 0))
    moved = jax.random.randint(jax.random.fold_in(own, 4), (amount // 2,), 0, 1 << 20) % (margin + 1)
    lengths = lengths.at[giver].add(-moved).at[receiver].add(moved)
    items = jnp.searchsorted(jnp.cumsum(lengths), jnp.arange(rows * top), side="right").astype(jnp.int32)
    listing = items.reshape(top, rows).T
    listing = listing[jax.random.permutation(jax.random.fold_in(own, 1), rows)]
    rotation = jax.random.randint(jax.random.fold_in(own, 2), (rows, 1), 0, top)
    return jnp.take_along_axis(listing, (jnp.arange(top)[None, :] + rotation) % top, axis=1)


def load_shares(number_of, total, reach, slope, full):
    weights = [(1 << 20) // math.isqrt(standing ** slope) + 1 for standing in range(1, number_of + 1)]
    largest = reach if full else min(reach, max(-(-total // number_of), total * weights[0] // sum(weights)))
    least = 1 if total - largest >= number_of - 1 else 0
    given, rest = [largest] + [least] * (number_of - 1), total - largest - least * (number_of - 1)
    while rest > 0:
        movable = [i for i in range(1, number_of) if given[i] < largest] or [i for i in range(1, number_of) if given[i] < reach]
        pool, budget = sum([weights[i] for i in movable]), rest
        for i in movable:
            addition = min(reach - given[i], max(1, budget * weights[i] // pool), rest)
            given[i] = given[i] + addition
            rest = rest - addition
    return np.array(given)


def scatter_about(stream_key, extent, deviation, limit, pieces=(), kind=jnp.bfloat16):
    entries = jax.random.normal(stream_key, extent, jnp.float32) * deviation
    if len(pieces) > 0:
        entries = levels(stream_key, extent, pieces, -0.22, 0.18) * entries
    return jnp.clip(entries, min=-limit, max=limit).astype(kind)


def setup_inputs(seed: int = 0, part: int = 0) -> dict:
    key_of = jax.random.split(jax.random.key(seed), 7)
    own_keys = jax.random.split(jax.random.fold_in(key_of[6], part), 7)
    traces = scatter_about(own_keys[0], (TRACES, BANDS * BAND), 1.0, 6.0, ((0, 16),))
    class_map_keys = jax.random.split(jax.random.fold_in(own_keys[1], 1), TRACES // TR_DEV)
    class_map_turns = jax.random.permutation(jax.random.fold_in(own_keys[1], 3), TRACES // TR_DEV)
    class_map = jax.vmap(lambda own, number: deal_out(jax.random.fold_in(own_keys[1], 2), own, number, TR_DEV, N_OFF, 1, CAP, 2))(class_map_keys, class_map_turns).reshape((TRACES, 1))
    mid_bins = with_ends(jax.random.randint(own_keys[2], (TRACES,), 0, MB), jax.random.fold_in(own_keys[2], 1), 0, MB - 1).astype(jnp.int32)
    fold_count = with_ends(jax.random.randint(own_keys[3], (CLASSES,), 1, 9), jax.random.fold_in(own_keys[3], 1), 1, 8).astype(jnp.int32)
    weight_tiles = scatter_about(key_of[4], (CLASSES, NPAT, BAND, PTS), (BAND * BANDS) ** -0.5, 0.09375, ((0, 4),))
    apertures = with_ends(jax.random.randint(own_keys[5], (TILES, BANDS), 0, NPAT + 1), jax.random.fold_in(own_keys[5], 1), 0, NPAT).astype(jnp.int32)
    return {"traces": traces, "class_map": class_map, "mid_bins": mid_bins, "fold_count": fold_count, "weight_tiles": weight_tiles, "apertures": apertures}


def migrate_column(col_traces, col_class, col_bins, col_pattern, fold_count, weight_tiles):
    keys = col_class * MB + col_bins
    stack = jax.ops.segment_sum(col_traces.astype(jnp.float32), keys, num_segments=CLASSES * MB)
    stack = stack.astype(jnp.bfloat16).reshape(CLASSES, MB, BANDS, BAND)
    select = (col_pattern[:, :, None] == jnp.arange(1, NPAT + 1, dtype=jnp.int32)[None, None, :]).astype(jnp.float32)
    inverse = 1.0 / fold_count.astype(jnp.float32)

    def one_class(total, items):
        class_stack, class_tiles, class_inv = items
        partial_value = jnp.einsum('mbs,ksp->kbmp', class_stack.astype(jnp.float32), class_tiles.astype(jnp.float32))
        term = jnp.einsum('gbk,kbmp->gmp', select, partial_value, precision=lax.Precision.HIGHEST)
        return total + term * class_inv, None

    start = jnp.zeros((N_OFF * TIL_DEV, MB, PTS), jnp.float32)
    total, _ = lax.scan(one_class, start, (stack, weight_tiles, inverse))
    return total


def reference(traces, class_map, mid_bins, fold_count, weight_tiles, apertures):
    width = BANDS * BAND
    col_traces = traces.reshape(N_OFF, N_TILE, TR_DEV, width).transpose(1, 0, 2, 3).reshape(N_TILE, N_OFF * TR_DEV, width)
    col_class = class_map[:, 0].reshape(N_OFF, N_TILE, TR_DEV).transpose(1, 0, 2).reshape(N_TILE, N_OFF * TR_DEV)
    col_bins = mid_bins.reshape(N_OFF, N_TILE, TR_DEV).transpose(1, 0, 2).reshape(N_TILE, N_OFF * TR_DEV)
    col_pattern = apertures.reshape(N_OFF, N_TILE, TIL_DEV, BANDS).transpose(1, 0, 2, 3).reshape(N_TILE, N_OFF * TIL_DEV, BANDS)

    def column(items):
        return migrate_column(items[0], items[1], items[2], items[3], fold_count, weight_tiles)

    images = lax.map(column, (col_traces, col_class, col_bins, col_pattern))
    images = images.reshape(N_TILE, N_OFF, TIL_DEV, MB, PTS).transpose(1, 0, 2, 3, 4)
    return images.reshape(N_OFF * N_TILE * TIL_DEV, MB, PTS)
```

```python
import functools

import jax
import jax.numpy as jnp
from jax import lax
from jax.experimental import pallas as pl
from jax.experimental.pallas import tpu as pltpu
from jax.sharding import PartitionSpec as P

BANDS = 32
BAND = 128
PTS = 128
MB = 128
NPAT = 4
SUB = 16
INFO = NPAT * BAND
F32 = jnp.float32
BF16 = jnp.bfloat16
VMEM = pl.BlockSpec(memory_space=pltpu.VMEM)
SMEM = pl.BlockSpec(memory_space=pltpu.SMEM)


def call(kernel, out, scratch=(), flops=0, moved=0):
    return functools.partial(
        pl.pallas_call,
        kernel,
        out_shape=out,
        scratch_shapes=scratch,
        compiler_params=pltpu.CompilerParams(vmem_limit_bytes=24 * 1024 * 1024),
        cost_estimate=pl.CostEstimate(flops=flops, bytes_accessed=moved, transcendentals=0),
    )


def pack_kernel(weight_ref, pattern_ref, fold_ref, packet_ref, info):
    tiles = pattern_ref.shape[0]
    packet_ref[0:INFO] = weight_ref[0].reshape(INFO, PTS)
    info[...] = jnp.zeros_like(info)
    info[0:tiles, 0:BANDS] = pattern_ref[...].astype(F32)
    info[tiles : tiles + 1] = jnp.full((1, PTS), fold_ref[0], jnp.int32).astype(F32)
    info[tiles + 1 : tiles + 2] = jnp.full((1, PTS), lax.axis_index("off"), jnp.int32).astype(F32)
    packet_ref[INFO:] = info[...].astype(BF16)


def band_sums(packet_ref, own_ref, near_ref, hi_ref, lo_ref, tiles):
    depth = BANDS * SUB
    pattern = packet_ref[INFO : INFO + SUB]
    band = lax.broadcasted_iota(jnp.int32, (PTS, depth), 0)
    column = lax.broadcasted_iota(jnp.int32, (PTS, depth), 1)
    spread = jnp.where(column // SUB == band, 1.0, 0.0).astype(BF16)
    wide = jnp.dot(pattern, spread, preferred_element_type=F32)
    row = lax.broadcasted_iota(jnp.int32, (NPAT * SUB, depth), 0)
    col = lax.broadcasted_iota(jnp.int32, (NPAT * SUB, depth), 1)
    value = (row // SUB + 1).astype(F32)
    same = row % SUB == col % SUB
    chosen = jnp.concatenate(
        [
            jnp.where(same & (jnp.broadcast_to(wide[g : g + 1], (NPAT * SUB, depth)) == value), 1.0, 0.0)
            for g in range(tiles)
        ],
        axis=0,
    ).astype(BF16)
    traces = own_ref.shape[0]
    for half, ref in enumerate((own_ref, near_ref)):
        for pair in range(traces // (2 * SUB)):
            at = pair * 2 * SUB
            block = jnp.concatenate(
                [
                    jnp.concatenate(
                        [
                            ref[at + n * SUB : at + (n + 1) * SUB, b * BAND : (b + 1) * BAND]
                            for n in range(2)
                        ],
                        axis=1,
                    )
                    for b in range(BANDS)
                ],
                axis=0,
            )
            sums = jnp.dot(chosen, block, preferred_element_type=F32)
            for n in range(2):
                for g in range(tiles):
                    for a in range(NPAT):
                        top = (g * NPAT + a) * SUB
                        slab = sums[top : top + SUB, n * BAND : (n + 1) * BAND]
                        hi = slab.astype(BF16)
                        lo = (slab - hi.astype(F32)).astype(BF16)
                        to = (g * 2 + half) * traces + at + n * SUB
                        hi_ref[to : to + SUB, a * BAND : (a + 1) * BAND] = hi
                        lo_ref[to : to + SUB, a * BAND : (a + 1) * BAND] = lo


def weigh(hi_ref, lo_ref, named, packets, tiles):
    total = None
    hi, lo = hi_ref[...], lo_ref[...]
    named = jnp.concatenate([named] * tiles, axis=0)
    for at in range(0, len(packets), 2):
        some = packets[at : at + 2]
        weights = jnp.concatenate([p[0:INFO] for p in some], axis=1) if len(some) > 1 else some[0][0:INFO]
        product = jnp.dot(hi, weights, preferred_element_type=F32) + jnp.dot(
            lo, weights, preferred_element_type=F32
        )
        for n, p in enumerate(some):
            info = p[INFO : INFO + SUB].astype(F32)
            scale = 1.0 / info[tiles : tiles + 1]
            mine = named == info[tiles + 1 : tiles + 2]
            part = jnp.where(mine, product[:, n * PTS : (n + 1) * PTS] * scale, 0.0)
            total = part if total is None else total + part
    return total


def bin_rows(total, binning, tiles):
    rows = binning.shape[1]
    wide = jnp.concatenate([total[g * rows : (g + 1) * rows] for g in range(tiles)], axis=1)
    hi = wide.astype(BF16)
    lo = (wide - hi.astype(F32)).astype(BF16)
    return jnp.dot(binning, hi, preferred_element_type=F32) + jnp.dot(
        binning, lo, preferred_element_type=F32
    )


def prepare_kernel(own_ref, near_ref, bins_ref, near_bins_ref, class_ref, near_class_ref,
                   packet_ref, near_packet_ref, binning_ref, named_ref, total_ref, hi_ref, lo_ref):
    tiles = hi_ref.shape[0] // named_ref.shape[0]
    traces = own_ref.shape[0]
    for half, (bins, classes) in enumerate(((bins_ref, class_ref), (near_bins_ref, near_class_ref))):
        at = half * traces
        place = lax.broadcasted_iota(jnp.int32, (MB, traces), 0)
        binning_ref[:, at : at + traces] = jnp.where(place == bins[...], 1.0, 0.0).astype(BF16)
        named_ref[at : at + traces] = jnp.broadcast_to(classes[...], (traces, traces)).astype(F32).T
    band_sums(packet_ref, own_ref, near_ref, hi_ref, lo_ref, tiles)
    total_ref[...] = weigh(hi_ref, lo_ref, named_ref[...], [packet_ref, near_packet_ref], tiles)


def begin_kernel(own_ref, near_ref, named_ref, pattern_ref, *refs):
    packets, (total_ref, hi_ref, lo_ref) = refs[:-3], refs[-3:]
    tiles = hi_ref.shape[0] // named_ref.shape[0]
    band_sums(pattern_ref, own_ref, near_ref, hi_ref, lo_ref, tiles)
    total_ref[...] = weigh(hi_ref, lo_ref, named_ref[...], packets, tiles)


def finish_kernel(total_ref, hi_ref, lo_ref, named_ref, binning_ref, *refs):
    packets, out_ref = refs[:-1], refs[-1]
    tiles = out_ref.shape[0]
    total = total_ref[...] + weigh(hi_ref, lo_ref, named_ref[...], packets, tiles)
    image = bin_rows(total, binning_ref[...], tiles)
    for g in range(tiles):
        out_ref[g] = image[:, g * PTS : (g + 1) * PTS].astype(out_ref.dtype)


def shards(traces, class_map, mid_bins, fold_count, weight_tiles, apertures):
    n_off = lax.axis_size("off")
    chips = n_off // 2
    tr_dev = traces.shape[0]
    tiles = apertures.shape[0]
    shape = jax.ShapeDtypeStruct

    def near(x):
        return lax.ppermute(x, "off", [(i, i ^ 1) for i in range(n_off)])

    def far(x, j):
        return lax.ppermute(
            x, "off", [(i, (i // 2 + j) % chips * 2 + i % 2) for i in range(n_off)]
        )

    packet = call(
        pack_kernel, shape((INFO + SUB, PTS), BF16), [pltpu.VMEM((SUB, PTS), F32)], moved=300000
    )(in_specs=[VMEM, VMEM, SMEM], out_specs=VMEM)(weight_tiles, apertures, fold_count)
    far_packets = [far(packet, j) for j in range(1, chips)]
    near_traces = near(traces)
    near_packet = near(packet)
    bins = mid_bins.reshape(1, tr_dev)
    classes = class_map.reshape(1, tr_dev)
    near_bins, near_classes = near(bins), near(classes)

    rows = 2 * tr_dev
    sums = shape((tiles * rows, NPAT * BAND), BF16)
    total = shape((tiles * rows, PTS), F32)
    work = 2 * tiles * rows * (NPAT * BAND) * PTS
    binning, named, own_total, own_hi, own_lo = call(
        prepare_kernel, (shape((MB, rows), BF16), shape((rows, PTS), F32), total, sums, sums),
        flops=10 * work, moved=8 << 20,
    )(in_specs=[VMEM] * 8, out_specs=[VMEM] * 5)(
        traces, near_traces, bins, near_bins, classes, near_classes, packet, near_packet
    )
    relayed = [near(p) for p in far_packets]
    received = []
    for j, p in enumerate(far_packets, 1):
        others = [packet, near_packet] + far_packets
        begun = call(begin_kernel, (total, sums, sums), flops=10 * work, moved=8 << 20)(
            in_specs=[VMEM] * (4 + len(others)), out_specs=[VMEM] * 3
        )(traces, near_traces, named, p, *others)
        part = call(finish_kernel, shape((tiles, MB, PTS), BF16), flops=4 * work, moved=2 << 20)(
            in_specs=[VMEM] * (5 + len(relayed)), out_specs=VMEM
        )(*begun, named, binning, *relayed)
        received.append(far(part, chips - j))
    rest = far_packets + relayed
    image = call(finish_kernel, shape((tiles, MB, PTS), F32), flops=6 * work, moved=2 << 20)(
        in_specs=[VMEM] * (5 + len(rest)), out_specs=VMEM
    )(own_total, own_hi, own_lo, named, binning, *rest)
    for part in received:
        image = image + part.astype(F32)
    return image


def solution(mesh):
    placed = (
        P(("grp", "off", "tile"), None),
        P(("grp", "off", "tile"), None),
        P(("grp", "off", "tile")),
        P(("grp", "off")),
        P("off", None, None, None),
        P(("grp", "off", "tile"), None),
    )
    return jax.shard_map(
        shards,
        mesh=mesh,
        in_specs=placed,
        out_specs=P(("grp", "off", "tile"), None, None),
        check_vma=False,
    )
```

```python
import functools

import jax
import jax.numpy as jnp
from jax import lax
from jax.experimental import pallas as pl
from jax.experimental.pallas import tpu as pltpu
from jax.sharding import PartitionSpec as P

BANDS = 32
BAND = 128
PTS = 128
MB = 128
NPAT = 4
SUB = 16
DEPTH = NPAT * BAND
F32 = jnp.float32
BF16 = jnp.bfloat16
VMEM = pl.BlockSpec(memory_space=pltpu.VMEM)
SMEM = pl.BlockSpec(memory_space=pltpu.SMEM)


def call(kernel, out, scratch=(), flops=0, moved=0, limit=24 << 20):
    return functools.partial(
        pl.pallas_call,
        kernel,
        out_shape=out,
        scratch_shapes=scratch,
        compiler_params=pltpu.CompilerParams(vmem_limit_bytes=limit),
        cost_estimate=pl.CostEstimate(flops=flops, bytes_accessed=moved, transcendentals=0),
    )


def zero_kernel(out_ref):
    out_ref[...] = jnp.zeros_like(out_ref)


def info_kernel(zero_ref, fold_ref, bins_ref, class_ref, pattern_ref, info_ref, info):
    info[...] = jnp.broadcast_to(zero_ref[0:1], info.shape)
    info[0:1] = jnp.full((1, PTS), fold_ref[0], jnp.int32).astype(F32)
    info[1:2] = bins_ref[...].astype(F32)
    info[2:3] = class_ref[...].astype(F32)
    info[8 : 8 + pattern_ref.shape[0], 0:BANDS] = pattern_ref[...].astype(F32)
    info_ref[...] = info[...].astype(BF16)


def owner(chips, j, turn):
    me = lax.axis_index("off")
    core = lax.rem(me, 2)
    chip = lax.rem(me // 2 + chips - j, chips)
    return chip * 2 + (1 - core if turn else core)


def choice(info, tiles):
    depth = BANDS * SUB
    band = lax.broadcasted_iota(jnp.int32, (PTS, depth), 0)
    column = lax.broadcasted_iota(jnp.int32, (PTS, depth), 1)
    spread = jnp.where(column // SUB == band, 1.0, 0.0).astype(BF16)
    wide = jnp.dot(info, spread, preferred_element_type=F32)[8:SUB]
    row = lax.broadcasted_iota(jnp.int32, (NPAT * SUB, depth), 0)
    col = lax.broadcasted_iota(jnp.int32, (NPAT * SUB, depth), 1)
    value = (row // SUB + 1).astype(F32)
    same = row % SUB == col % SUB
    return jnp.concatenate(
        [
            jnp.where(same & (jnp.broadcast_to(wide[g : g + 1], (NPAT * SUB, depth)) == value), 1.0, 0.0)
            for g in range(tiles)
        ],
        axis=0,
    ).astype(BF16)


def band_sums(chosen, own_ref, near_ref, hi_ref, lo_ref, tiles):
    traces = own_ref.shape[0]
    for half, ref in enumerate((own_ref, near_ref)):
        for pair in range(traces // (2 * SUB)):
            at = pair * 2 * SUB
            block = jnp.concatenate(
                [
                    jnp.concatenate(
                        [
                            ref[at + n * SUB : at + (n + 1) * SUB, b * BAND : (b + 1) * BAND]
                            for n in range(2)
                        ],
                        axis=1,
                    )
                    for b in range(BANDS)
                ],
                axis=0,
            )
            sums = jnp.dot(chosen, block, preferred_element_type=F32)
            for n in range(2):
                for g in range(tiles):
                    for a in range(NPAT):
                        top = (g * NPAT + a) * SUB
                        slab = sums[top : top + SUB, n * BAND : (n + 1) * BAND]
                        hi = slab.astype(BF16)
                        lo = (slab - hi.astype(F32)).astype(BF16)
                        to = (g * 2 + half) * traces + at + n * SUB
                        hi_ref[to : to + SUB, a * BAND : (a + 1) * BAND] = hi
                        lo_ref[to : to + SUB, a * BAND : (a + 1) * BAND] = lo


def weigh(hi_ref, lo_ref, named, weights, owners, tiles):
    total = None
    hi, lo = hi_ref[...], lo_ref[...]
    named = jnp.concatenate([named] * tiles, axis=0)
    for at in range(0, len(weights), 2):
        some = [w[...] for w in weights[at : at + 2]]
        wide = jnp.concatenate(some, axis=1) if len(some) > 1 else some[0]
        product = jnp.dot(hi, wide, preferred_element_type=F32) + jnp.dot(
            lo, wide, preferred_element_type=F32
        )
        for n in range(len(some)):
            mine = named == owners[at + n].astype(F32)
            part = jnp.where(mine, product[:, n * PTS : (n + 1) * PTS], 0.0)
            total = part if total is None else total + part
    return total


def over_fold(named, infos, owners):
    scale = jnp.zeros_like(named)
    for info, held in zip(infos, owners):
        scale = jnp.where(named == held.astype(F32), 1.0 / info[0:SUB].astype(F32)[0:1], scale)
    return scale


def bin_rows(total, binning, tiles):
    rows = binning.shape[1]
    wide = jnp.concatenate([total[g * rows : (g + 1) * rows] for g in range(tiles)], axis=1)
    hi = wide.astype(BF16)
    lo = (wide - hi.astype(F32)).astype(BF16)
    return jnp.dot(binning, hi, preferred_element_type=F32) + jnp.dot(
        binning, lo, preferred_element_type=F32
    )


def choice_kernel(info_ref, near_info_ref, *refs):
    infos, (chosen_ref, binning_ref, named_ref) = refs[:-3], refs[-3:]
    traces = named_ref.shape[0] // 2
    for half, ref in enumerate((info_ref, near_info_ref)):
        at = half * traces
        info = ref[...].astype(F32)
        place = lax.broadcasted_iota(jnp.int32, (MB, traces), 0).astype(F32)
        binning_ref[:, at : at + traces] = jnp.where(place == info[1:2], 1.0, 0.0).astype(BF16)
        named_ref[at : at + traces] = jnp.broadcast_to(info[2:3], (traces, traces)).T
    infos = (info_ref,) + infos
    size = chosen_ref.shape[0] // len(infos)
    for n, info in enumerate(infos):
        chosen_ref[n * size : (n + 1) * size] = choice(info[...], size // (NPAT * SUB))


def begin_kernel(chips, j, own_ref, near_ref, named_ref, chosen_ref, *refs):
    weights, (total_ref, hi_ref, lo_ref) = refs[:-3], refs[-3:]
    tiles = hi_ref.shape[0] // named_ref.shape[0]
    size = tiles * NPAT * SUB
    band_sums(chosen_ref[j * size : (j + 1) * size], own_ref, near_ref, hi_ref, lo_ref, tiles)
    owners = [owner(chips, 0, 0), owner(chips, 0, 1)] + [owner(chips, n, 0) for n in range(1, chips)]
    total_ref[...] = weigh(hi_ref, lo_ref, named_ref[...], weights, owners, tiles)


def image_of(total, named, binning, infos, owners, out_ref):
    tiles = out_ref.shape[0]
    total = total * jnp.concatenate([over_fold(named, infos, owners)] * tiles, axis=0)
    image = bin_rows(total, binning, tiles)
    for g in range(tiles):
        out_ref[g] = image[:, g * PTS : (g + 1) * PTS].astype(out_ref.dtype)


def all_owners(chips):
    return [owner(chips, n, turn) for turn in range(2) for n in range(chips)]


def finish_kernel(chips, hi_ref, lo_ref, total_ref, named_ref, binning_ref, *refs):
    infos, weights, out_ref = refs[: 2 * chips], refs[2 * chips : -1], refs[-1]
    named, owners = named_ref[...], all_owners(chips)
    total = total_ref[...] + weigh(
        hi_ref, lo_ref, named, weights, owners[chips + 1 :], out_ref.shape[0]
    )
    image_of(total, named, binning_ref[...], infos, owners, out_ref)


def own_kernel(chips, own_ref, near_ref, chosen_ref, named_ref, binning_ref, *refs):
    infos, weights, (out_ref, hi_ref, lo_ref) = refs[: 2 * chips], refs[2 * chips : -3], refs[-3:]
    named, owners, tiles = named_ref[...], all_owners(chips), out_ref.shape[0]
    band_sums(chosen_ref[0 : tiles * NPAT * SUB], own_ref, near_ref, hi_ref, lo_ref, tiles)
    total = weigh(hi_ref, lo_ref, named, weights, owners, tiles)
    image_of(total, named, binning_ref[...], infos, owners, out_ref)


def shards(traces, class_map, mid_bins, fold_count, weight_tiles, apertures):
    n_off = lax.axis_size("off")
    chips = n_off // 2
    tr_dev = traces.shape[0]
    tiles = apertures.shape[0]
    shape = jax.ShapeDtypeStruct

    def near(x):
        return lax.ppermute(x, "off", [(i, i ^ 1) for i in range(n_off)])

    def far(x, j, turn=0):
        return lax.ppermute(
            x, "off", [(i, (i // 2 + j) % chips * 2 + (i % 2 ^ turn)) for i in range(n_off)]
        )

    hops = range(1, chips)
    weights = weight_tiles.reshape(DEPTH, PTS)
    zero = call(zero_kernel, shape((8, PTS), F32), flops=5 * 10**9)(in_specs=[], out_specs=VMEM)()
    fold_count, zero = lax.optimization_barrier((fold_count, zero))
    info = call(info_kernel, shape((SUB, PTS), BF16), [pltpu.VMEM((SUB, PTS), F32)], flops=5 * 10**9)(
        in_specs=[VMEM, SMEM, VMEM, VMEM, VMEM], out_specs=VMEM
    )(zero, fold_count, mid_bins.reshape(1, tr_dev), class_map.reshape(1, tr_dev), apertures)
    far_weights = [far(weights, j) for j in hops]
    far_infos = [far(info, j) for j in hops]
    near_traces, near_weights, near_info = near(traces), near(weights), near(info)

    rows = 2 * tr_dev
    sums = shape((tiles * rows, NPAT * BAND), BF16)
    total = shape((tiles * rows, PTS), F32)
    work = 2 * tiles * rows * (NPAT * BAND) * PTS
    chosen, binning, named = call(
        choice_kernel,
        (shape((chips * tiles * NPAT * SUB, BANDS * SUB), BF16), shape((MB, rows), BF16),
         shape((rows, PTS), F32)),
    )(in_specs=[VMEM] * (1 + chips), out_specs=[VMEM] * 3)(info, near_info, *far_infos)
    far_weights, chosen = lax.optimization_barrier((far_weights, chosen))
    relayed = [near(w) for w in far_weights]
    infos = [info] + far_infos + [near_info] + [near(x) for x in far_infos]
    received = []
    for j in hops:
        others = [weights, near_weights] + far_weights
        begun, *its_sums = call(functools.partial(begin_kernel, chips, j), (total, sums, sums))(
            in_specs=[VMEM] * (4 + len(others)), out_specs=[VMEM] * 3
        )(traces, near_traces, named, chosen, *others)
        rest = [begun, named, binning] + infos + relayed
        part = call(functools.partial(finish_kernel, chips), shape((tiles, MB, PTS), BF16))(
            in_specs=[VMEM] * (2 + len(rest)), out_specs=VMEM
        )(*its_sums, *rest)
        received.append(far(part, chips - j))
    rest = infos + [weights] + far_weights + [near_weights] + relayed
    image = call(
        functools.partial(own_kernel, chips), shape((tiles, MB, PTS), F32),
        [pltpu.VMEM(sums.shape, BF16)] * 2, flops=15 * work,
    )(in_specs=[VMEM] * (5 + len(rest)), out_specs=VMEM)(
        traces, near_traces, chosen, named, binning, *rest
    )
    for part in received:
        image = image + part.astype(F32)
    return image


def solution(mesh):
    placed = (
        P(("grp", "off", "tile"), None),
        P(("grp", "off", "tile"), None),
        P(("grp", "off", "tile")),
        P(("grp", "off")),
        P("off", None, None, None),
        P(("grp", "off", "tile"), None),
    )
    return jax.shard_map(
        shards,
        mesh=mesh,
        in_specs=placed,
        out_specs=P(("grp", "off", "tile"), None, None),
        check_vma=False,
    )
```

```python
import functools

import jax
import jax.numpy as jnp
from jax import lax
from jax.experimental import pallas as pl
from jax.experimental.pallas import tpu as pltpu
from jax.sharding import PartitionSpec as P

BANDS = 32
BAND = 128
PTS = 128
MB = 128
NPAT = 4
SUB = 16
DEPTH = NPAT * BAND
INFO_COST = 5 * 10**8
BEGIN_COST = 11 * 10**8
SUMS_COST = 4 * 10**8
FACTS_COST = 10**9
F32 = jnp.float32
BF16 = jnp.bfloat16
VMEM = pl.BlockSpec(memory_space=pltpu.VMEM)
ANY = pl.BlockSpec(memory_space=pl.ANY)
SMEM = pl.BlockSpec(memory_space=pltpu.SMEM)


def call(kernel, out, scratch=(), flops=0, moved=0, limit=24 << 20):
    return functools.partial(
        pl.pallas_call,
        kernel,
        out_shape=out,
        scratch_shapes=scratch,
        compiler_params=pltpu.CompilerParams(vmem_limit_bytes=limit),
        cost_estimate=pl.CostEstimate(flops=flops, bytes_accessed=moved, transcendentals=0),
    )


def facts_kernel(fold_ref, pattern_ref, facts_ref, facts):
    facts[...] = jnp.zeros_like(facts)
    facts[0:1] = jnp.full((1, PTS), fold_ref[0], jnp.int32).astype(F32)
    facts[8 : 8 + pattern_ref.shape[0], 0:BANDS] = pattern_ref[...].astype(F32)
    facts_ref[...] = facts[...].astype(BF16)


def info_kernel(after_ref, facts_ref, bins_ref, class_ref, info_ref, info):
    info[...] = facts_ref[...].astype(F32)
    info[1:2] = bins_ref[...].astype(F32)
    info[2:3] = class_ref[...].astype(F32)
    info_ref[...] = info[...].astype(BF16)


def owner(chips, j, turn):
    me = lax.axis_index("off")
    core = lax.rem(me, 2)
    chip = lax.rem(me // 2 + chips - j, chips)
    return chip * 2 + (1 - core if turn else core)


def choice(pattern):
    depth = BANDS * SUB
    tiles = pattern.shape[0]
    band = lax.broadcasted_iota(jnp.int32, (BANDS, depth), 0)
    column = lax.broadcasted_iota(jnp.int32, (BANDS, depth), 1)
    spread = jnp.where(column // SUB == band, 1.0, 0.0).astype(BF16)
    padded = jnp.concatenate([pattern] * (8 // tiles), axis=0).astype(BF16)
    wide = jnp.dot(padded, spread, preferred_element_type=F32)
    row = lax.broadcasted_iota(jnp.int32, (NPAT * SUB, depth), 0)
    col = lax.broadcasted_iota(jnp.int32, (NPAT * SUB, depth), 1)
    value = (row // SUB + 1).astype(F32)
    same = row % SUB == col % SUB
    return jnp.concatenate(
        [
            jnp.where(same & (jnp.broadcast_to(wide[g : g + 1], (NPAT * SUB, depth)) == value), 1.0, 0.0)
            for g in range(tiles)
        ],
        axis=0,
    ).astype(BF16)


def band_sums(chosen, own_ref, near_ref, hi_ref, lo_ref, tiles):
    traces = own_ref.shape[0]
    for half, ref in enumerate((own_ref, near_ref)):
        for pair in range(traces // (2 * SUB)):
            at = pair * 2 * SUB
            block = jnp.concatenate(
                [
                    jnp.concatenate(
                        [
                            ref[at + n * SUB : at + (n + 1) * SUB, b * BAND : (b + 1) * BAND]
                            for n in range(2)
                        ],
                        axis=1,
                    )
                    for b in range(BANDS)
                ],
                axis=0,
            )
            sums = jnp.dot(chosen, block, preferred_element_type=F32)
            for n in range(2):
                for g in range(tiles):
                    for a in range(NPAT):
                        top = (g * NPAT + a) * SUB
                        slab = sums[top : top + SUB, n * BAND : (n + 1) * BAND]
                        hi = slab.astype(BF16)
                        lo = (slab - hi.astype(F32)).astype(BF16)
                        to = (g * 2 + half) * traces + at + n * SUB
                        hi_ref[to : to + SUB, a * BAND : (a + 1) * BAND] = hi
                        lo_ref[to : to + SUB, a * BAND : (a + 1) * BAND] = lo


def weigh(hi_ref, lo_ref, named, weights, owners, tiles):
    total = None
    hi, lo = hi_ref[...], lo_ref[...]
    named = jnp.concatenate([named] * tiles, axis=0)
    for at in range(0, len(weights), 2):
        some = [w[0:DEPTH] for w in weights[at : at + 2]]
        wide = jnp.concatenate(some, axis=1) if len(some) > 1 else some[0]
        product = jnp.dot(hi, wide, preferred_element_type=F32) + jnp.dot(
            lo, wide, preferred_element_type=F32
        )
        for n in range(len(some)):
            mine = named == owners[at + n].astype(F32)
            part = jnp.where(mine, product[:, n * PTS : (n + 1) * PTS], 0.0)
            total = part if total is None else total + part
    return total


def over_fold(named, infos, owners):
    scale = jnp.zeros_like(named)
    for info, held in zip(infos, owners):
        scale = jnp.where(named == held.astype(F32), 1.0 / info[...].astype(F32)[0:1], scale)
    return scale


def bin_rows(total, binning, tiles):
    rows = binning.shape[1]
    wide = jnp.concatenate([total[g * rows : (g + 1) * rows] for g in range(tiles)], axis=1)
    hi = wide.astype(BF16)
    lo = (wide - hi.astype(F32)).astype(BF16)
    return jnp.dot(binning, hi, preferred_element_type=F32) + jnp.dot(
        binning, lo, preferred_element_type=F32
    )


def sums_kernel(own_ref, near_ref, facts_ref, hi_ref, lo_ref):
    tiles = hi_ref.shape[0] // (2 * own_ref.shape[0])
    chosen = choice(facts_ref[...].astype(F32)[8 : 8 + tiles, 0:BANDS])
    band_sums(chosen, own_ref, near_ref, hi_ref, lo_ref, tiles)


def begin_kernel(chips, hi_ref, lo_ref, weight_ref, near_weight_ref, *refs):
    infos, (total_ref, scale_ref, named_ref, binning_ref) = refs[:-4], refs[-4:]
    traces = named_ref.shape[0] // 2
    for half in range(2):
        at = half * traces
        info = infos[half * chips][...].astype(F32)
        place = lax.broadcasted_iota(jnp.int32, (MB, traces), 0).astype(F32)
        binning_ref[:, at : at + traces] = jnp.where(place == info[1:2], 1.0, 0.0).astype(BF16)
        named_ref[at : at + traces] = jnp.broadcast_to(info[2:3], (traces, traces)).T
    named, tiles = named_ref[...], hi_ref.shape[0] // named_ref.shape[0]
    owners = [owner(chips, 0, 0), owner(chips, 0, 1)]
    total_ref[...] = weigh(hi_ref, lo_ref, named, [weight_ref, near_weight_ref], owners, tiles)
    scale_ref[...] = over_fold(named, infos, all_owners(chips))


def image_of(total, scale, binning, out_ref):
    tiles = out_ref.shape[0]
    total = total * jnp.concatenate([scale] * tiles, axis=0)
    image = bin_rows(total, binning, tiles)
    for g in range(tiles):
        out_ref[g] = image[:, g * PTS : (g + 1) * PTS].astype(out_ref.dtype)


def all_owners(chips):
    return [owner(chips, n, turn) for turn in range(2) for n in range(chips)]


def finish_kernel(chips, hi_ref, lo_ref, total_ref, named_ref, scale_ref, binning_ref, *refs):
    weights, out_ref = refs[:-1], refs[-1]
    owners = [owner(chips, n, turn) for turn in range(2) for n in range(1, chips)]
    total = total_ref[...] + weigh(hi_ref, lo_ref, named_ref[...], weights, owners, out_ref.shape[0])
    image_of(total, scale_ref[...], binning_ref[...], out_ref)


def own_kernel(chips, own_ref, near_ref, pattern_ref, named_ref, scale_ref, binning_ref, *refs):
    weights, (out_ref, hi_ref, lo_ref) = refs[:-3], refs[-3:]
    tiles = out_ref.shape[0]
    chosen = choice(pattern_ref[...].astype(F32))
    band_sums(chosen, own_ref, near_ref, hi_ref, lo_ref, tiles)
    total = weigh(hi_ref, lo_ref, named_ref[...], weights, all_owners(chips), tiles)
    image_of(total, scale_ref[...], binning_ref[...], out_ref)


def shards(traces, class_map, mid_bins, fold_count, weight_tiles, apertures):
    n_off = lax.axis_size("off")
    chips = n_off // 2
    tr_dev = traces.shape[0]
    tiles = apertures.shape[0]
    shape = jax.ShapeDtypeStruct

    def near(x):
        return lax.ppermute(x, "off", [(i, i ^ 1) for i in range(n_off)])

    def far(x, j, turn=0):
        return lax.ppermute(
            x, "off", [(i, (i // 2 + j) % chips * 2 + (i % 2 ^ turn)) for i in range(n_off)]
        )

    hops = range(1, chips)
    weights = weight_tiles.reshape(DEPTH, PTS)
    far_weights = [far(weights, j) for j in hops]
    block = shape((SUB, PTS), BF16)
    facts = call(facts_kernel, block, [pltpu.VMEM(block.shape, F32)], flops=FACTS_COST)(
        in_specs=[SMEM, VMEM], out_specs=VMEM
    )(fold_count, apertures)
    far_facts = [far(facts, j) for j in hops]
    cross_facts = [far(facts, j, 1) for j in hops]
    near_traces, near_weights = near(traces), near(weights)
    info = call(info_kernel, block, [pltpu.VMEM(block.shape, F32)], flops=INFO_COST)(
        in_specs=[ANY] + [VMEM] * 3, out_specs=VMEM
    )(near_traces, facts, mid_bins.reshape(1, tr_dev), class_map.reshape(1, tr_dev))
    near_info = near(info)

    rows = 2 * tr_dev
    sums = shape((tiles * rows, NPAT * BAND), BF16)
    total = shape((tiles * rows, PTS), F32)
    by_row = shape((rows, PTS), F32)
    work = 2 * tiles * rows * (NPAT * BAND) * PTS
    far_weights, info = lax.optimization_barrier((far_weights, info))
    relayed = [near(w) for w in far_weights]
    infos = [info] + far_facts + [near_info] + cross_facts
    all_begun = []
    for j in hops:
        its_sums = call(sums_kernel, (sums, sums), flops=SUMS_COST)(
            in_specs=[VMEM] * 3, out_specs=[VMEM] * 2
        )(traces, near_traces, far_facts[j - 1])
        begun, scale, named, binning = call(
            functools.partial(begin_kernel, chips),
            (total, by_row, by_row, shape((MB, rows), BF16)), flops=BEGIN_COST,
        )(in_specs=[VMEM] * (4 + len(infos)), out_specs=[VMEM] * 4)(
            *its_sums, weights, near_weights, *infos
        )
        all_begun.append((begun, *its_sums))
    received = []
    for j in hops:
        begun, *its_sums = all_begun[j - 1]
        rest = [begun, named, scale, binning] + far_weights + relayed
        part = call(functools.partial(finish_kernel, chips), shape((tiles, MB, PTS), BF16))(
            in_specs=[VMEM] * (2 + len(rest)), out_specs=VMEM
        )(*its_sums, *rest)
        received.append(far(part, chips - j))
    rest = [weights] + far_weights + [near_weights] + relayed
    image = call(
        functools.partial(own_kernel, chips), shape((tiles, MB, PTS), F32),
        [pltpu.VMEM(sums.shape, BF16)] * 2, flops=15 * work,
    )(in_specs=[VMEM] * (6 + len(rest)), out_specs=VMEM)(
        traces, near_traces, apertures, named, scale, binning, *rest
    )
    for part in received:
        image = image + part.astype(F32)
    return image


def solution(mesh):
    placed = (
        P(("grp", "off", "tile"), None),
        P(("grp", "off", "tile"), None),
        P(("grp", "off", "tile")),
        P(("grp", "off")),
        P("off", None, None, None),
        P(("grp", "off", "tile"), None),
    )
    return jax.shard_map(
        shards,
        mesh=mesh,
        in_specs=placed,
        out_specs=P(("grp", "off", "tile"), None, None),
        check_vma=False,
    )
```

```python
import functools

import jax
import jax.numpy as jnp
from jax import lax
from jax.experimental import pallas as pl
from jax.experimental.pallas import tpu as pltpu
from jax.sharding import PartitionSpec as P

BANDS = 32
BAND = 128
PTS = 128
MB = 128
NPAT = 4
SUB = 16
DEPTH = NPAT * BAND
INFO_COST = 7 * 10**8
BEGIN_COST = 11 * 10**8
SUMS_COST = 0
FACTS_COST = 15 * 10**7
CHOICE_COST = 7 * 10**9
RELAY_COST = 4 * 10**9
F32 = jnp.float32
BF16 = jnp.bfloat16
VMEM = pl.BlockSpec(memory_space=pltpu.VMEM)
ANY = pl.BlockSpec(memory_space=pl.ANY)
SMEM = pl.BlockSpec(memory_space=pltpu.SMEM)


def call(kernel, out, scratch=(), flops=0, moved=0, limit=24 << 20):
    return functools.partial(
        pl.pallas_call,
        kernel,
        out_shape=out,
        scratch_shapes=scratch,
        compiler_params=pltpu.CompilerParams(vmem_limit_bytes=limit),
        cost_estimate=pl.CostEstimate(flops=flops, bytes_accessed=moved, transcendentals=0),
    )


def facts_kernel(fold_ref, pattern_ref, facts_ref, facts):
    facts[...] = jnp.zeros_like(facts)
    facts[0:1] = jnp.full((1, PTS), fold_ref[0], jnp.int32).astype(F32)
    facts[8 : 8 + pattern_ref.shape[0], 0:BANDS] = pattern_ref[...].astype(F32)
    facts_ref[...] = facts[...].astype(BF16)


def packet_kernel(facts_ref, weight_ref, bins_ref, class_ref, packet_ref, again_ref, info):
    packet_ref[0:DEPTH] = weight_ref[...]
    info[...] = facts_ref[...].astype(F32)
    info[1:2] = bins_ref[...].astype(F32)
    info[2:3] = class_ref[...].astype(F32)
    packet_ref[DEPTH:] = info[...].astype(BF16)
    again_ref[...] = facts_ref[...]


def owner(chips, j, turn):
    me = lax.axis_index("off")
    core = lax.rem(me, 2)
    chip = lax.rem(me // 2 + chips - j, chips)
    return chip * 2 + (1 - core if turn else core)


def choice(pattern):
    depth = BANDS * SUB
    tiles = pattern.shape[0]
    band = lax.broadcasted_iota(jnp.int32, (BANDS, depth), 0)
    column = lax.broadcasted_iota(jnp.int32, (BANDS, depth), 1)
    spread = jnp.where(column // SUB == band, 1.0, 0.0).astype(BF16)
    padded = jnp.concatenate([pattern] * (8 // tiles), axis=0).astype(BF16)
    wide = jnp.dot(padded, spread, preferred_element_type=F32)
    row = lax.broadcasted_iota(jnp.int32, (NPAT * SUB, depth), 0)
    col = lax.broadcasted_iota(jnp.int32, (NPAT * SUB, depth), 1)
    value = (row // SUB + 1).astype(F32)
    same = row % SUB == col % SUB
    return jnp.concatenate(
        [
            jnp.where(same & (jnp.broadcast_to(wide[g : g + 1], (NPAT * SUB, depth)) == value), 1.0, 0.0)
            for g in range(tiles)
        ],
        axis=0,
    ).astype(BF16)


def band_sums(chosen, own_ref, near_ref, hi_ref, lo_ref, tiles):
    traces = own_ref.shape[0]
    for half, ref in enumerate((own_ref, near_ref)):
        for pair in range(traces // (2 * SUB)):
            at = pair * 2 * SUB
            block = jnp.concatenate(
                [
                    jnp.concatenate(
                        [
                            ref[at + n * SUB : at + (n + 1) * SUB, b * BAND : (b + 1) * BAND]
                            for n in range(2)
                        ],
                        axis=1,
                    )
                    for b in range(BANDS)
                ],
                axis=0,
            )
            sums = jnp.dot(chosen, block, preferred_element_type=F32)
            for n in range(2):
                for g in range(tiles):
                    for a in range(NPAT):
                        top = (g * NPAT + a) * SUB
                        slab = sums[top : top + SUB, n * BAND : (n + 1) * BAND]
                        hi = slab.astype(BF16)
                        lo = (slab - hi.astype(F32)).astype(BF16)
                        to = (g * 2 + half) * traces + at + n * SUB
                        hi_ref[to : to + SUB, a * BAND : (a + 1) * BAND] = hi
                        lo_ref[to : to + SUB, a * BAND : (a + 1) * BAND] = lo


def weigh(hi_ref, lo_ref, named, weights, owners, tiles):
    total = None
    hi, lo = hi_ref[...], lo_ref[...]
    named = jnp.concatenate([named] * tiles, axis=0)
    for at in range(0, len(weights), 2):
        some = [w[0:DEPTH] for w in weights[at : at + 2]]
        wide = jnp.concatenate(some, axis=1) if len(some) > 1 else some[0]
        product = jnp.dot(hi, wide, preferred_element_type=F32) + jnp.dot(
            lo, wide, preferred_element_type=F32
        )
        for n in range(len(some)):
            mine = named == owners[at + n].astype(F32)
            part = jnp.where(mine, product[:, n * PTS : (n + 1) * PTS], 0.0)
            total = part if total is None else total + part
    return total


def over_fold(named, infos, owners):
    scale = jnp.zeros_like(named)
    for info, held in zip(infos, owners):
        scale = jnp.where(named == held.astype(F32), 1.0 / info[info.shape[0] - SUB :].astype(F32)[0:1], scale)
    return scale


def bin_rows(total, binning, tiles):
    rows = binning.shape[1]
    wide = jnp.concatenate([total[g * rows : (g + 1) * rows] for g in range(tiles)], axis=1)
    hi = wide.astype(BF16)
    lo = (wide - hi.astype(F32)).astype(BF16)
    return jnp.dot(binning, hi, preferred_element_type=F32) + jnp.dot(
        binning, lo, preferred_element_type=F32
    )


def choice_kernel(after_ref, facts_ref, chosen_ref):
    tiles = chosen_ref.shape[0] // (NPAT * SUB)
    chosen_ref[...] = choice(facts_ref[...].astype(F32)[8 : 8 + tiles, 0:BANDS])


def sums_kernel(own_ref, near_ref, chosen_ref, hi_ref, lo_ref):
    tiles = hi_ref.shape[0] // (2 * own_ref.shape[0])
    band_sums(chosen_ref[...], own_ref, near_ref, hi_ref, lo_ref, tiles)


def relay_kernel(after_ref, also_ref, weight_ref, out_ref):
    out_ref[...] = weight_ref[...]


def begin_kernel(chips, hi_ref, lo_ref, *refs):
    infos, (total_ref, scale_ref, named_ref, binning_ref) = refs[:-4], refs[-4:]
    traces = named_ref.shape[0] // 2
    for half in range(2):
        at = half * traces
        info = infos[half * chips][DEPTH:].astype(F32)
        place = lax.broadcasted_iota(jnp.int32, (MB, traces), 0).astype(F32)
        binning_ref[:, at : at + traces] = jnp.where(place == info[1:2], 1.0, 0.0).astype(BF16)
        named_ref[at : at + traces] = jnp.broadcast_to(info[2:3], (traces, traces)).T
    named, tiles = named_ref[...], hi_ref.shape[0] // named_ref.shape[0]
    owners = [owner(chips, 0, 0), owner(chips, 0, 1)]
    total_ref[...] = weigh(hi_ref, lo_ref, named, [infos[0], infos[chips]], owners, tiles)
    scale_ref[...] = over_fold(named, infos, all_owners(chips))


def image_of(total, scale, binning, out_ref):
    tiles = out_ref.shape[0]
    total = total * jnp.concatenate([scale] * tiles, axis=0)
    image = bin_rows(total, binning, tiles)
    for g in range(tiles):
        out_ref[g] = image[:, g * PTS : (g + 1) * PTS].astype(out_ref.dtype)


def all_owners(chips):
    return [owner(chips, n, turn) for turn in range(2) for n in range(chips)]


def finish_kernel(chips, hi_ref, lo_ref, total_ref, named_ref, scale_ref, binning_ref, *refs):
    weights, out_ref = refs[:-1], refs[-1]
    owners = [owner(chips, n, turn) for turn in range(2) for n in range(1, chips)]
    total = total_ref[...] + weigh(hi_ref, lo_ref, named_ref[...], weights, owners, out_ref.shape[0])
    image_of(total, scale_ref[...], binning_ref[...], out_ref)


def own_kernel(chips, own_ref, near_ref, pattern_ref, named_ref, scale_ref, binning_ref, *refs):
    weights, (out_ref, hi_ref, lo_ref) = refs[:-3], refs[-3:]
    tiles = out_ref.shape[0]
    chosen = choice(pattern_ref[...].astype(F32))
    band_sums(chosen, own_ref, near_ref, hi_ref, lo_ref, tiles)
    total = weigh(hi_ref, lo_ref, named_ref[...], weights, all_owners(chips), tiles)
    image_of(total, scale_ref[...], binning_ref[...], out_ref)


def shards(traces, class_map, mid_bins, fold_count, weight_tiles, apertures):
    n_off = lax.axis_size("off")
    chips = n_off // 2
    tr_dev = traces.shape[0]
    tiles = apertures.shape[0]
    shape = jax.ShapeDtypeStruct

    def near(x):
        return lax.ppermute(x, "off", [(i, i ^ 1) for i in range(n_off)])

    def far(x, j, turn=0):
        return lax.ppermute(
            x, "off", [(i, (i // 2 + j) % chips * 2 + (i % 2 ^ turn)) for i in range(n_off)]
        )

    hops = range(1, chips)
    weights = weight_tiles.reshape(DEPTH, PTS)
    far_weights = [far(weights, j) for j in hops]
    block = shape((SUB, PTS), BF16)
    facts = call(facts_kernel, block, [pltpu.VMEM(block.shape, F32)], flops=FACTS_COST)(
        in_specs=[SMEM, VMEM], out_specs=VMEM
    )(fold_count, apertures)
    far_facts = [far(facts, j) for j in hops]
    tied, _ = lax.optimization_barrier((traces, facts))
    near_traces = near(tied)
    packet, again = call(
        packet_kernel, (shape((DEPTH + SUB, PTS), BF16), block), [pltpu.VMEM(block.shape, F32)], flops=INFO_COST
    )(in_specs=[VMEM] * 4, out_specs=[VMEM] * 2)(
        facts, weights, mid_bins.reshape(1, tr_dev), class_map.reshape(1, tr_dev)
    )
    near_packet = near(packet)
    cross_facts = [far(again, j, 1) for j in hops]

    rows = 2 * tr_dev
    sums = shape((tiles * rows, NPAT * BAND), BF16)
    total = shape((tiles * rows, PTS), F32)
    by_row = shape((rows, PTS), F32)
    work = 2 * tiles * rows * (NPAT * BAND) * PTS
    relayed = [
        near(call(relay_kernel, shape(w.shape, BF16), flops=RELAY_COST)(
            in_specs=[ANY, VMEM, VMEM], out_specs=VMEM
        )(packet, traces, w))
        for w in far_weights
    ]
    infos = [packet] + far_facts + [near_packet] + cross_facts
    all_begun = []
    for j in hops:
        chosen = call(choice_kernel, shape((tiles * NPAT * SUB, BANDS * SUB), BF16), flops=CHOICE_COST)(
            in_specs=[VMEM] * 2, out_specs=VMEM
        )(traces, far_facts[j - 1])
        its_sums = call(sums_kernel, (sums, sums), flops=SUMS_COST)(
            in_specs=[VMEM] * 3, out_specs=[VMEM] * 2
        )(traces, near_traces, chosen)
        begun, scale, named, binning = call(
            functools.partial(begin_kernel, chips),
            (total, by_row, by_row, shape((MB, rows), BF16)), flops=BEGIN_COST,
        )(in_specs=[VMEM] * (2 + len(infos)), out_specs=[VMEM] * 4)(*its_sums, *infos)
        all_begun.append((begun, *its_sums))
    received = []
    for j in hops:
        begun, *its_sums = all_begun[j - 1]
        rest = [begun, named, scale, binning] + far_weights + relayed
        part = call(functools.partial(finish_kernel, chips), shape((tiles, MB, PTS), BF16))(
            in_specs=[VMEM] * (2 + len(rest)), out_specs=VMEM
        )(*its_sums, *rest)
        received.append(far(part, chips - j))
    rest = [packet] + far_weights + [near_packet] + relayed
    image = call(
        functools.partial(own_kernel, chips), shape((tiles, MB, PTS), F32),
        [pltpu.VMEM(sums.shape, BF16)] * 2, flops=15 * work,
    )(in_specs=[VMEM] * (6 + len(rest)), out_specs=VMEM)(
        traces, near_traces, apertures, named, scale, binning, *rest
    )
    for part in received:
        image = image + part.astype(F32)
    return image


def solution(mesh):
    placed = (
        P(("grp", "off", "tile"), None),
        P(("grp", "off", "tile"), None),
        P(("grp", "off", "tile")),
        P(("grp", "off")),
        P("off", None, None, None),
        P(("grp", "off", "tile"), None),
    )
    return jax.shard_map(
        shards,
        mesh=mesh,
        in_specs=placed,
        out_specs=P(("grp", "off", "tile"), None, None),
        check_vma=False,
    )
```

```python
import functools

import jax
import jax.numpy as jnp
from jax import lax
from jax.experimental import pallas as pl
from jax.experimental.pallas import tpu as pltpu
from jax.sharding import PartitionSpec as P

BANDS = 32
BAND = 128
PTS = 128
MB = 128
NPAT = 4
SUB = 16
DEPTH = NPAT * BAND
INFO_COST = 55 * 10**7
BEGIN_COST = 8 * 10**8
FACTS_COST = 2 * 10**8
CHOICE_COST = 6 * 10**9
RELAY_COST = 5 * 10**9
F32 = jnp.float32
BF16 = jnp.bfloat16
VMEM = pl.BlockSpec(memory_space=pltpu.VMEM)
ANY = pl.BlockSpec(memory_space=pl.ANY)
SMEM = pl.BlockSpec(memory_space=pltpu.SMEM)


def call(kernel, out, scratch=(), flops=0, moved=0, limit=24 << 20):
    return functools.partial(
        pl.pallas_call,
        kernel,
        out_shape=out,
        scratch_shapes=scratch,
        compiler_params=pltpu.CompilerParams(vmem_limit_bytes=limit),
        cost_estimate=pl.CostEstimate(flops=flops, bytes_accessed=moved, transcendentals=0),
    )


def facts_kernel(fold_ref, pattern_ref, facts_ref, facts):
    facts[...] = jnp.zeros_like(facts)
    facts[0:1] = jnp.full((1, PTS), fold_ref[0], jnp.int32).astype(F32)
    facts[8 : 8 + pattern_ref.shape[0], 0:BANDS] = pattern_ref[...].astype(F32)
    facts_ref[...] = facts[...].astype(BF16)


def packet_kernel(facts_ref, weight_ref, bins_ref, class_ref, packet_ref, again_ref, info):
    packet_ref[0:DEPTH] = weight_ref[...]
    info[...] = facts_ref[...].astype(F32)
    info[1:2] = bins_ref[...].astype(F32)
    info[2:3] = class_ref[...].astype(F32)
    packet_ref[DEPTH:] = info[...].astype(BF16)
    again_ref[...] = facts_ref[...]


def owner(chips, j, turn):
    me = lax.axis_index("off")
    core = lax.rem(me, 2)
    chip = lax.rem(me // 2 + chips - j, chips)
    return chip * 2 + (1 - core if turn else core)


def choice(pattern):
    depth = BANDS * SUB
    tiles = pattern.shape[0]
    band = lax.broadcasted_iota(jnp.int32, (BANDS, depth), 0)
    column = lax.broadcasted_iota(jnp.int32, (BANDS, depth), 1)
    spread = jnp.where(column // SUB == band, 1.0, 0.0).astype(BF16)
    padded = jnp.concatenate([pattern] * (8 // tiles), axis=0).astype(BF16)
    wide = jnp.dot(padded, spread, preferred_element_type=F32)
    row = lax.broadcasted_iota(jnp.int32, (NPAT * SUB, depth), 0)
    col = lax.broadcasted_iota(jnp.int32, (NPAT * SUB, depth), 1)
    value = (row // SUB + 1).astype(F32)
    same = row % SUB == col % SUB
    return jnp.concatenate(
        [
            jnp.where(same & (jnp.broadcast_to(wide[g : g + 1], (NPAT * SUB, depth)) == value), 1.0, 0.0)
            for g in range(tiles)
        ],
        axis=0,
    ).astype(BF16)


def band_sums(chosen, own_ref, near_ref, hi_ref, lo_ref, tiles):
    traces = own_ref.shape[0]
    for half, ref in enumerate((own_ref, near_ref)):
        for pair in range(traces // (2 * SUB)):
            at = pair * 2 * SUB
            block = jnp.concatenate(
                [
                    jnp.concatenate(
                        [
                            ref[at + n * SUB : at + (n + 1) * SUB, b * BAND : (b + 1) * BAND]
                            for n in range(2)
                        ],
                        axis=1,
                    )
                    for b in range(BANDS)
                ],
                axis=0,
            )
            sums = jnp.dot(chosen, block, preferred_element_type=F32)
            for n in range(2):
                for g in range(tiles):
                    for a in range(NPAT):
                        top = (g * NPAT + a) * SUB
                        slab = sums[top : top + SUB, n * BAND : (n + 1) * BAND]
                        hi = slab.astype(BF16)
                        lo = (slab - hi.astype(F32)).astype(BF16)
                        to = (g * 2 + half) * traces + at + n * SUB
                        hi_ref[to : to + SUB, a * BAND : (a + 1) * BAND] = hi
                        lo_ref[to : to + SUB, a * BAND : (a + 1) * BAND] = lo


def weigh(hi_ref, lo_ref, named, weights, owners, tiles):
    total = None
    hi, lo = hi_ref[...], lo_ref[...]
    named = jnp.concatenate([named] * tiles, axis=0)
    for at in range(0, len(weights), 2):
        some = [w[0:DEPTH] for w in weights[at : at + 2]]
        wide = jnp.concatenate(some, axis=1) if len(some) > 1 else some[0]
        product = jnp.dot(hi, wide, preferred_element_type=F32) + jnp.dot(
            lo, wide, preferred_element_type=F32
        )
        for n in range(len(some)):
            mine = named == owners[at + n].astype(F32)
            part = jnp.where(mine, product[:, n * PTS : (n + 1) * PTS], 0.0)
            total = part if total is None else total + part
    return total


def over_fold(named, folds, owners):
    scale = jnp.zeros_like(named)
    for fold, held in zip(folds, owners):
        scale = jnp.where(named == held.astype(F32), 1.0 / fold, scale)
    return scale


def bin_rows(total, binning, tiles):
    rows = binning.shape[1]
    wide = jnp.concatenate([total[g * rows : (g + 1) * rows] for g in range(tiles)], axis=1)
    hi = wide.astype(BF16)
    lo = (wide - hi.astype(F32)).astype(BF16)
    return jnp.dot(binning, hi, preferred_element_type=F32) + jnp.dot(
        binning, lo, preferred_element_type=F32
    )


def facts_in_kernel(after_ref, facts_ref, out_ref):
    out_ref[...] = facts_ref[...]


def relay_kernel(after_ref, also_ref, weight_ref, out_ref):
    out_ref[...] = weight_ref[...]


def sums_kernel(own_ref, near_ref, facts_ref, hi_ref, lo_ref):
    tiles = hi_ref.shape[0] // (2 * own_ref.shape[0])
    chosen = choice(facts_ref[...].astype(F32)[8 : 8 + tiles, 0:BANDS])
    band_sums(chosen, own_ref, near_ref, hi_ref, lo_ref, tiles)


def begin_kernel(chips, hi_ref, lo_ref, packet_ref, near_packet_ref, *refs):
    facts, (total_ref, scale_ref, named_ref, binning_ref) = refs[:-4], refs[-4:]
    traces = named_ref.shape[0] // 2
    tiles = hi_ref.shape[0] // (2 * traces)
    folds = []
    for half, ref in enumerate((packet_ref, near_packet_ref)):
        at = half * traces
        info = ref[DEPTH:].astype(F32)
        place = lax.broadcasted_iota(jnp.int32, (MB, traces), 0).astype(F32)
        binning_ref[:, at : at + traces] = jnp.where(place == info[1:2], 1.0, 0.0).astype(BF16)
        named_ref[at : at + traces] = jnp.broadcast_to(info[2:3], (traces, traces)).T
        folds.append(info[0:1])
        for n in range(half * (chips - 1), (half + 1) * (chips - 1)):
            folds.append(facts[n][...].astype(F32)[0:1])
    named = named_ref[...]
    owners = [owner(chips, 0, 0), owner(chips, 0, 1)]
    total_ref[...] = weigh(hi_ref, lo_ref, named, [packet_ref, near_packet_ref], owners, tiles)
    scale_ref[...] = over_fold(named, folds, all_owners(chips))


def image_of(total, scale, binning, out_ref):
    tiles = out_ref.shape[0]
    total = total * jnp.concatenate([scale] * tiles, axis=0)
    image = bin_rows(total, binning, tiles)
    for g in range(tiles):
        out_ref[g] = image[:, g * PTS : (g + 1) * PTS].astype(out_ref.dtype)


def all_owners(chips):
    return [owner(chips, n, turn) for turn in range(2) for n in range(chips)]


def finish_kernel(chips, hi_ref, lo_ref, total_ref, named_ref, scale_ref, binning_ref, *refs):
    weights, out_ref = refs[:-1], refs[-1]
    owners = [owner(chips, n, turn) for turn in range(2) for n in range(1, chips)]
    total = total_ref[...] + weigh(hi_ref, lo_ref, named_ref[...], weights, owners, out_ref.shape[0])
    image_of(total, scale_ref[...], binning_ref[...], out_ref)


def own_kernel(chips, own_ref, near_ref, pattern_ref, named_ref, scale_ref, binning_ref, *refs):
    weights, (out_ref, hi_ref, lo_ref) = refs[:-3], refs[-3:]
    tiles = out_ref.shape[0]
    chosen = choice(pattern_ref[...].astype(F32))
    band_sums(chosen, own_ref, near_ref, hi_ref, lo_ref, tiles)
    total = weigh(hi_ref, lo_ref, named_ref[...], weights, all_owners(chips), tiles)
    image_of(total, scale_ref[...], binning_ref[...], out_ref)


def shards(traces, class_map, mid_bins, fold_count, weight_tiles, apertures):
    n_off = lax.axis_size("off")
    chips = n_off // 2
    tr_dev = traces.shape[0]
    tiles = apertures.shape[0]
    shape = jax.ShapeDtypeStruct

    def near(x):
        return lax.ppermute(x, "off", [(i, i ^ 1) for i in range(n_off)])

    def far(x, j, turn=0):
        return lax.ppermute(
            x, "off", [(i, (i // 2 + j) % chips * 2 + (i % 2 ^ turn)) for i in range(n_off)]
        )

    hops = range(1, chips)
    weights = weight_tiles.reshape(DEPTH, PTS)
    far_weights = [far(weights, j) for j in hops]
    block = shape((SUB, PTS), BF16)
    facts = call(facts_kernel, block, [pltpu.VMEM(block.shape, F32)], flops=FACTS_COST)(
        in_specs=[SMEM, VMEM], out_specs=VMEM
    )(fold_count, apertures)
    far_facts = [far(facts, j) for j in hops]
    tied, _ = lax.optimization_barrier((traces, facts))
    near_traces = near(tied)
    packet, again = call(
        packet_kernel, (shape((DEPTH + SUB, PTS), BF16), block), [pltpu.VMEM(block.shape, F32)], flops=INFO_COST
    )(in_specs=[VMEM] * 4, out_specs=[VMEM] * 2)(
        facts, weights, mid_bins.reshape(1, tr_dev), class_map.reshape(1, tr_dev)
    )
    near_packet = near(packet)
    cross_facts = [far(again, j, 1) for j in hops]

    rows = 2 * tr_dev
    sums = shape((tiles * rows, NPAT * BAND), BF16)
    total = shape((tiles * rows, PTS), F32)
    by_row = shape((rows, PTS), F32)
    work = 2 * tiles * rows * (NPAT * BAND) * PTS
    relayed = [
        near(call(relay_kernel, shape(w.shape, BF16), flops=RELAY_COST)(
            in_specs=[ANY, VMEM, VMEM], out_specs=VMEM
        )(packet, traces, w))
        for w in far_weights
    ]
    known = [
        call(facts_in_kernel, block, flops=CHOICE_COST)(in_specs=[VMEM] * 2, out_specs=VMEM)(traces, x)
        for x in far_facts
    ] + cross_facts
    all_begun = []
    for j in hops:
        its_sums = call(sums_kernel, (sums, sums))(in_specs=[VMEM] * 3, out_specs=[VMEM] * 2)(
            traces, near_traces, known[j - 1]
        )
        begun, scale, named, binning = call(
            functools.partial(begin_kernel, chips),
            (total, by_row, by_row, shape((MB, rows), BF16)), flops=BEGIN_COST,
        )(in_specs=[VMEM] * (4 + len(known)), out_specs=[VMEM] * 4)(
            *its_sums, packet, near_packet, *known
        )
        all_begun.append((begun, *its_sums))
    received = []
    for j in hops:
        begun, *its_sums = all_begun[j - 1]
        rest = [begun, named, scale, binning] + far_weights + relayed
        part = call(functools.partial(finish_kernel, chips), shape((tiles, MB, PTS), BF16))(
            in_specs=[VMEM] * (2 + len(rest)), out_specs=VMEM
        )(*its_sums, *rest)
        received.append(far(part, chips - j))
    rest = [packet] + far_weights + [near_packet] + relayed
    image = call(
        functools.partial(own_kernel, chips), shape((tiles, MB, PTS), F32),
        [pltpu.VMEM(sums.shape, BF16)] * 2, flops=15 * work,
    )(in_specs=[VMEM] * (6 + len(rest)), out_specs=VMEM)(
        traces, near_traces, apertures, named, scale, binning, *rest
    )
    for part in received:
        image = image + part.astype(F32)
    return image


def solution(mesh):
    placed = (
        P(("grp", "off", "tile"), None),
        P(("grp", "off", "tile"), None),
        P(("grp", "off", "tile")),
        P(("grp", "off")),
        P("off", None, None, None),
        P(("grp", "off", "tile"), None),
    )
    return jax.shard_map(
        shards,
        mesh=mesh,
        in_specs=placed,
        out_specs=P(("grp", "off", "tile"), None, None),
        check_vma=False,
    )
```

```python
import functools

import jax
import jax.numpy as jnp
from jax import lax
from jax.experimental import pallas as pl
from jax.experimental.pallas import tpu as pltpu
from jax.sharding import PartitionSpec as P

BANDS = 32
BAND = 128
PTS = 128
MB = 128
NPAT = 4
SUB = 16
DEPTH = NPAT * BAND
INFO_COST = 55 * 10**7
SCALE_COST = 8 * 10**8
FACTS_COST = 2 * 10**8
NEWS_COST = 6 * 10**9
RELAY_COST = 5 * 10**9
F32 = jnp.float32
BF16 = jnp.bfloat16
VMEM = pl.BlockSpec(memory_space=pltpu.VMEM)
ANY = pl.BlockSpec(memory_space=pl.ANY)
SMEM = pl.BlockSpec(memory_space=pltpu.SMEM)


def call(kernel, out, scratch=(), flops=0, moved=0, limit=24 << 20):
    return functools.partial(
        pl.pallas_call,
        kernel,
        out_shape=out,
        scratch_shapes=scratch,
        compiler_params=pltpu.CompilerParams(vmem_limit_bytes=limit),
        cost_estimate=pl.CostEstimate(flops=flops, bytes_accessed=moved, transcendentals=0),
    )


def facts_kernel(fold_ref, pattern_ref, facts_ref, facts):
    facts[...] = jnp.zeros_like(facts)
    facts[0:1] = jnp.full((1, PTS), fold_ref[0], jnp.int32).astype(F32)
    facts[8 : 8 + pattern_ref.shape[0], 0:BANDS] = pattern_ref[...].astype(F32)
    facts_ref[...] = facts[...].astype(BF16)


def packet_kernel(facts_ref, weight_ref, bins_ref, class_ref, packet_ref, again_ref, info):
    packet_ref[0:DEPTH] = weight_ref[...]
    info[...] = facts_ref[...].astype(F32)
    info[1:2] = bins_ref[...].astype(F32)
    info[2:3] = class_ref[...].astype(F32)
    packet_ref[DEPTH:] = info[...].astype(BF16)
    again_ref[...] = facts_ref[...]


def owner(chips, j, turn):
    me = lax.axis_index("off")
    core = lax.rem(me, 2)
    chip = lax.rem(me // 2 + chips - j, chips)
    return chip * 2 + (1 - core if turn else core)


def choice(pattern):
    depth = BANDS * SUB
    tiles = pattern.shape[0]
    band = lax.broadcasted_iota(jnp.int32, (BANDS, depth), 0)
    column = lax.broadcasted_iota(jnp.int32, (BANDS, depth), 1)
    spread = jnp.where(column // SUB == band, 1.0, 0.0).astype(BF16)
    padded = jnp.concatenate([pattern] * (8 // tiles), axis=0).astype(BF16)
    wide = jnp.dot(padded, spread, preferred_element_type=F32)
    row = lax.broadcasted_iota(jnp.int32, (NPAT * SUB, depth), 0)
    col = lax.broadcasted_iota(jnp.int32, (NPAT * SUB, depth), 1)
    value = (row // SUB + 1).astype(F32)
    same = row % SUB == col % SUB
    return jnp.concatenate(
        [
            jnp.where(same & (jnp.broadcast_to(wide[g : g + 1], (NPAT * SUB, depth)) == value), 1.0, 0.0)
            for g in range(tiles)
        ],
        axis=0,
    ).astype(BF16)


def band_sums(chosen, own_ref, near_ref, hi_ref, lo_ref, tiles):
    traces = own_ref.shape[0]
    for half, ref in enumerate((own_ref, near_ref)):
        for pair in range(traces // (2 * SUB)):
            at = pair * 2 * SUB
            block = jnp.concatenate(
                [
                    jnp.concatenate(
                        [
                            ref[at + n * SUB : at + (n + 1) * SUB, b * BAND : (b + 1) * BAND]
                            for n in range(2)
                        ],
                        axis=1,
                    )
                    for b in range(BANDS)
                ],
                axis=0,
            )
            sums = jnp.dot(chosen, block, preferred_element_type=F32)
            for n in range(2):
                for g in range(tiles):
                    for a in range(NPAT):
                        top = (g * NPAT + a) * SUB
                        slab = sums[top : top + SUB, n * BAND : (n + 1) * BAND]
                        hi = slab.astype(BF16)
                        lo = (slab - hi.astype(F32)).astype(BF16)
                        to = (g * 2 + half) * traces + at + n * SUB
                        hi_ref[to : to + SUB, a * BAND : (a + 1) * BAND] = hi
                        lo_ref[to : to + SUB, a * BAND : (a + 1) * BAND] = lo


def weigh(hi_ref, lo_ref, named, weights, owners, tiles):
    total = None
    hi, lo = hi_ref[...], lo_ref[...]
    named = jnp.concatenate([named] * tiles, axis=0)
    for at in range(0, len(weights), 2):
        some = [w[0:DEPTH] for w in weights[at : at + 2]]
        wide = jnp.concatenate(some, axis=1) if len(some) > 1 else some[0]
        product = jnp.dot(hi, wide, preferred_element_type=F32) + jnp.dot(
            lo, wide, preferred_element_type=F32
        )
        for n in range(len(some)):
            mine = named == owners[at + n].astype(F32)
            part = jnp.where(mine, product[:, n * PTS : (n + 1) * PTS], 0.0)
            total = part if total is None else total + part
    return total


def over_fold(named, folds, owners):
    scale = jnp.zeros_like(named)
    for fold, held in zip(folds, owners):
        scale = jnp.where(named == held.astype(F32), 1.0 / fold, scale)
    return scale


def bin_rows(total, binning, tiles):
    rows = binning.shape[1]
    wide = jnp.concatenate([total[g * rows : (g + 1) * rows] for g in range(tiles)], axis=1)
    hi = wide.astype(BF16)
    lo = (wide - hi.astype(F32)).astype(BF16)
    return jnp.dot(binning, hi, preferred_element_type=F32) + jnp.dot(
        binning, lo, preferred_element_type=F32
    )


def facts_in_kernel(after_ref, facts_ref, out_ref):
    out_ref[...] = facts_ref[...]


def relay_kernel(after_ref, also_ref, weight_ref, out_ref):
    out_ref[...] = weight_ref[...]


def begin_kernel(chips, own_ref, near_ref, facts_ref, packet_ref, near_packet_ref,
                 total_ref, hi_ref, lo_ref, named_ref, binning_ref):
    traces = own_ref.shape[0]
    tiles = hi_ref.shape[0] // (2 * traces)
    chosen = choice(facts_ref[...].astype(F32)[8 : 8 + tiles, 0:BANDS])
    band_sums(chosen, own_ref, near_ref, hi_ref, lo_ref, tiles)
    for half, ref in enumerate((packet_ref, near_packet_ref)):
        at = half * traces
        info = ref[DEPTH:].astype(F32)
        place = lax.broadcasted_iota(jnp.int32, (MB, traces), 0).astype(F32)
        binning_ref[:, at : at + traces] = jnp.where(place == info[1:2], 1.0, 0.0).astype(BF16)
        named_ref[at : at + traces] = jnp.broadcast_to(info[2:3], (traces, traces)).T
    owners = [owner(chips, 0, 0), owner(chips, 0, 1)]
    weights = [packet_ref, near_packet_ref]
    total_ref[...] = weigh(hi_ref, lo_ref, named_ref[...], weights, owners, tiles)


def scale_kernel(chips, named_ref, packet_ref, near_packet_ref, *refs):
    facts, scale_ref = refs[:-1], refs[-1]
    folds = []
    for half, ref in enumerate((packet_ref, near_packet_ref)):
        folds.append(ref[DEPTH:].astype(F32)[0:1])
        for n in range(half * (chips - 1), (half + 1) * (chips - 1)):
            folds.append(facts[n][...].astype(F32)[0:1])
    scale_ref[...] = over_fold(named_ref[...], folds, all_owners(chips))


def image_of(total, scale, binning, out_ref):
    tiles = out_ref.shape[0]
    total = total * jnp.concatenate([scale] * tiles, axis=0)
    image = bin_rows(total, binning, tiles)
    for g in range(tiles):
        out_ref[g] = image[:, g * PTS : (g + 1) * PTS].astype(out_ref.dtype)


def all_owners(chips):
    return [owner(chips, n, turn) for turn in range(2) for n in range(chips)]


def finish_kernel(chips, hi_ref, lo_ref, total_ref, named_ref, scale_ref, binning_ref, *refs):
    weights, out_ref = refs[:-1], refs[-1]
    owners = [owner(chips, n, turn) for turn in range(2) for n in range(1, chips)]
    total = total_ref[...] + weigh(hi_ref, lo_ref, named_ref[...], weights, owners, out_ref.shape[0])
    image_of(total, scale_ref[...], binning_ref[...], out_ref)


def own_kernel(chips, own_ref, near_ref, pattern_ref, named_ref, scale_ref, binning_ref, *refs):
    weights, (out_ref, hi_ref, lo_ref) = refs[:-3], refs[-3:]
    tiles = out_ref.shape[0]
    chosen = choice(pattern_ref[...].astype(F32))
    band_sums(chosen, own_ref, near_ref, hi_ref, lo_ref, tiles)
    total = weigh(hi_ref, lo_ref, named_ref[...], weights, all_owners(chips), tiles)
    image_of(total, scale_ref[...], binning_ref[...], out_ref)


def shards(traces, class_map, mid_bins, fold_count, weight_tiles, apertures):
    n_off = lax.axis_size("off")
    chips = n_off // 2
    tr_dev = traces.shape[0]
    tiles = apertures.shape[0]
    shape = jax.ShapeDtypeStruct

    def near(x):
        return lax.ppermute(x, "off", [(i, i ^ 1) for i in range(n_off)])

    def far(x, j, turn=0):
        return lax.ppermute(
            x, "off", [(i, (i // 2 + j) % chips * 2 + (i % 2 ^ turn)) for i in range(n_off)]
        )

    hops = range(1, chips)
    weights = weight_tiles.reshape(DEPTH, PTS)
    far_weights = [far(weights, j) for j in hops]
    block = shape((SUB, PTS), BF16)
    facts = call(facts_kernel, block, [pltpu.VMEM(block.shape, F32)], flops=FACTS_COST)(
        in_specs=[SMEM, VMEM], out_specs=VMEM
    )(fold_count, apertures)
    far_facts = [far(facts, j) for j in hops]
    tied, _ = lax.optimization_barrier((traces, facts))
    near_traces = near(tied)
    packet, again = call(
        packet_kernel, (shape((DEPTH + SUB, PTS), BF16), block), [pltpu.VMEM(block.shape, F32)], flops=INFO_COST
    )(in_specs=[VMEM] * 4, out_specs=[VMEM] * 2)(
        facts, weights, mid_bins.reshape(1, tr_dev), class_map.reshape(1, tr_dev)
    )
    near_packet = near(packet)
    cross_facts = [far(again, j, 1) for j in hops]

    rows = 2 * tr_dev
    sums = shape((tiles * rows, NPAT * BAND), BF16)
    total = shape((tiles * rows, PTS), F32)
    by_row = shape((rows, PTS), F32)
    work = 2 * tiles * rows * (NPAT * BAND) * PTS
    relayed = [
        near(call(relay_kernel, shape(w.shape, BF16), flops=RELAY_COST)(
            in_specs=[ANY, VMEM, VMEM], out_specs=VMEM
        )(packet, traces, w))
        for w in far_weights
    ]
    known = [
        call(facts_in_kernel, block, flops=NEWS_COST)(in_specs=[VMEM] * 2, out_specs=VMEM)(traces, x)
        for x in far_facts
    ] + cross_facts
    all_begun = []
    for j in hops:
        begun, *its_sums, named, binning = call(
            functools.partial(begin_kernel, chips),
            (total, sums, sums, by_row, shape((MB, rows), BF16)),
        )(in_specs=[VMEM] * 5, out_specs=[VMEM] * 5)(
            traces, near_traces, known[j - 1], packet, near_packet
        )
        all_begun.append((begun, *its_sums))
    scale = call(functools.partial(scale_kernel, chips), by_row, flops=SCALE_COST)(
        in_specs=[VMEM] * (3 + len(known)), out_specs=VMEM
    )(named, packet, near_packet, *known)
    received = []
    for j in hops:
        begun, *its_sums = all_begun[j - 1]
        rest = [begun, named, scale, binning] + far_weights + relayed
        part = call(functools.partial(finish_kernel, chips), shape((tiles, MB, PTS), BF16))(
            in_specs=[VMEM] * (2 + len(rest)), out_specs=VMEM
        )(*its_sums, *rest)
        received.append(far(part, chips - j))
    rest = [packet] + far_weights + [near_packet] + relayed
    image = call(
        functools.partial(own_kernel, chips), shape((tiles, MB, PTS), F32),
        [pltpu.VMEM(sums.shape, BF16)] * 2, flops=15 * work,
    )(in_specs=[VMEM] * (6 + len(rest)), out_specs=VMEM)(
        traces, near_traces, apertures, named, scale, binning, *rest
    )
    for part in received:
        image = image + part.astype(F32)
    return image


def solution(mesh):
    placed = (
        P(("grp", "off", "tile"), None),
        P(("grp", "off", "tile"), None),
        P(("grp", "off", "tile")),
        P(("grp", "off")),
        P("off", None, None, None),
        P(("grp", "off", "tile"), None),
    )
    return jax.shard_map(
        shards,
        mesh=mesh,
        in_specs=placed,
        out_specs=P(("grp", "off", "tile"), None, None),
        check_vma=False,
    )
```

```python
import functools

import jax
import jax.numpy as jnp
from jax import lax
from jax.experimental import pallas as pl
from jax.experimental.pallas import tpu as pltpu
from jax.sharding import PartitionSpec as P

BANDS = 32
BAND = 128
PTS = 128
MB = 128
NPAT = 4
SUB = 16
DEPTH = NPAT * BAND
INFO_COST = 55 * 10**7
SCALE_COST = 8 * 10**8
FACTS_COST = 2 * 10**8
NEWS_COST = 6 * 10**9
RELAY_COST = 5 * 10**9
F32 = jnp.float32
BF16 = jnp.bfloat16
VMEM = pl.BlockSpec(memory_space=pltpu.VMEM)
ANY = pl.BlockSpec(memory_space=pl.ANY)
SMEM = pl.BlockSpec(memory_space=pltpu.SMEM)


def call(kernel, out, scratch=(), flops=0, moved=0, limit=24 << 20):
    return functools.partial(
        pl.pallas_call,
        kernel,
        out_shape=out,
        scratch_shapes=scratch,
        compiler_params=pltpu.CompilerParams(vmem_limit_bytes=limit),
        cost_estimate=pl.CostEstimate(flops=flops, bytes_accessed=moved, transcendentals=0),
    )


def facts_kernel(fold_ref, pattern_ref, facts_ref, facts):
    facts[...] = jnp.zeros_like(facts)
    facts[0:1] = jnp.full((1, PTS), fold_ref[0], jnp.int32).astype(F32)
    facts[8 : 8 + pattern_ref.shape[0], 0:BANDS] = pattern_ref[...].astype(F32)
    facts_ref[...] = facts[...].astype(BF16)


def packet_kernel(facts_ref, weight_ref, bins_ref, class_ref,
                  packet_ref, again_ref, spread_ref, code_ref, info):
    packet_ref[0:DEPTH] = weight_ref[...]
    info[...] = facts_ref[...].astype(F32)
    info[1:2] = bins_ref[...].astype(F32)
    info[2:3] = class_ref[...].astype(F32)
    packet_ref[DEPTH:] = info[...].astype(BF16)
    again_ref[...] = facts_ref[...]
    masks(spread_ref, code_ref)


def owner(chips, j, turn):
    me = lax.axis_index("off")
    core = lax.rem(me, 2)
    chip = lax.rem(me // 2 + chips - j, chips)
    return chip * 2 + (1 - core if turn else core)


def masks(spread_ref, code_ref):
    shape = spread_ref.shape
    band = lax.broadcasted_iota(jnp.int32, shape, 0)
    column = lax.broadcasted_iota(jnp.int32, shape, 1)
    spread_ref[...] = jnp.where(column // SUB == band, 1.0, 0.0).astype(BF16)
    row = lax.broadcasted_iota(jnp.int32, code_ref.shape, 0)
    col = lax.broadcasted_iota(jnp.int32, code_ref.shape, 1)
    code_ref[...] = jnp.where(row % SUB == col % SUB, (row // SUB + 1).astype(F32), -1.0)


def choice(pattern, spread, code):
    tiles = pattern.shape[0]
    padded = jnp.concatenate([pattern] * (8 // tiles), axis=0).astype(BF16)
    wide = jnp.dot(padded, spread, preferred_element_type=F32)
    return jnp.concatenate(
        [
            jnp.where(jnp.broadcast_to(wide[g : g + 1], code.shape) == code, 1.0, 0.0)
            for g in range(tiles)
        ],
        axis=0,
    ).astype(BF16)


def band_sums(chosen, own_ref, near_ref, hi_ref, lo_ref, tiles):
    traces = own_ref.shape[0]
    for half, ref in enumerate((own_ref, near_ref)):
        for pair in range(traces // (2 * SUB)):
            at = pair * 2 * SUB
            block = jnp.concatenate(
                [
                    jnp.concatenate(
                        [
                            ref[at + n * SUB : at + (n + 1) * SUB, b * BAND : (b + 1) * BAND]
                            for n in range(2)
                        ],
                        axis=1,
                    )
                    for b in range(BANDS)
                ],
                axis=0,
            )
            sums = jnp.dot(chosen, block, preferred_element_type=F32)
            for n in range(2):
                for g in range(tiles):
                    for a in range(NPAT):
                        top = (g * NPAT + a) * SUB
                        slab = sums[top : top + SUB, n * BAND : (n + 1) * BAND]
                        hi = slab.astype(BF16)
                        lo = (slab - hi.astype(F32)).astype(BF16)
                        to = (g * 2 + half) * traces + at + n * SUB
                        hi_ref[to : to + SUB, a * BAND : (a + 1) * BAND] = hi
                        lo_ref[to : to + SUB, a * BAND : (a + 1) * BAND] = lo


def weigh(hi_ref, lo_ref, named, weights, owners, tiles):
    total = None
    hi, lo = hi_ref[...], lo_ref[...]
    named = jnp.concatenate([named] * tiles, axis=0)
    for at in range(0, len(weights), 2):
        some = [w[0:DEPTH] for w in weights[at : at + 2]]
        wide = jnp.concatenate(some, axis=1) if len(some) > 1 else some[0]
        product = jnp.dot(hi, wide, preferred_element_type=F32) + jnp.dot(
            lo, wide, preferred_element_type=F32
        )
        for n in range(len(some)):
            mine = named == owners[at + n].astype(F32)
            part = jnp.where(mine, product[:, n * PTS : (n + 1) * PTS], 0.0)
            total = part if total is None else total + part
    return total


def over_fold(named, folds, owners):
    scale = jnp.zeros_like(named)
    for fold, held in zip(folds, owners):
        scale = jnp.where(named == held.astype(F32), 1.0 / fold, scale)
    return scale


def bin_rows(total, binning, tiles):
    rows = binning.shape[1]
    wide = jnp.concatenate([total[g * rows : (g + 1) * rows] for g in range(tiles)], axis=1)
    hi = wide.astype(BF16)
    lo = (wide - hi.astype(F32)).astype(BF16)
    return jnp.dot(binning, hi, preferred_element_type=F32) + jnp.dot(
        binning, lo, preferred_element_type=F32
    )


def facts_in_kernel(after_ref, facts_ref, out_ref):
    out_ref[...] = facts_ref[...]


def relay_kernel(after_ref, also_ref, weight_ref, out_ref):
    out_ref[...] = weight_ref[...]


def begin_kernel(chips, own_ref, near_ref, facts_ref, packet_ref, near_packet_ref, spread_ref, code_ref,
                 total_ref, hi_ref, lo_ref, named_ref, binning_ref):
    traces = own_ref.shape[0]
    tiles = hi_ref.shape[0] // (2 * traces)
    chosen = choice(facts_ref[...].astype(F32)[8 : 8 + tiles, 0:BANDS], spread_ref[...], code_ref[...])
    band_sums(chosen, own_ref, near_ref, hi_ref, lo_ref, tiles)
    for half, ref in enumerate((packet_ref, near_packet_ref)):
        at = half * traces
        info = ref[DEPTH:].astype(F32)
        place = lax.broadcasted_iota(jnp.int32, (MB, traces), 0).astype(F32)
        binning_ref[:, at : at + traces] = jnp.where(place == info[1:2], 1.0, 0.0).astype(BF16)
        named_ref[at : at + traces] = jnp.broadcast_to(info[2:3], (traces, traces)).T
    owners = [owner(chips, 0, 0), owner(chips, 0, 1)]
    weights = [packet_ref, near_packet_ref]
    total_ref[...] = weigh(hi_ref, lo_ref, named_ref[...], weights, owners, tiles)


def scale_kernel(chips, named_ref, packet_ref, near_packet_ref, *refs):
    facts, scale_ref = refs[:-1], refs[-1]
    folds = []
    for half, ref in enumerate((packet_ref, near_packet_ref)):
        folds.append(ref[DEPTH:].astype(F32)[0:1])
        for n in range(half * (chips - 1), (half + 1) * (chips - 1)):
            folds.append(facts[n][...].astype(F32)[0:1])
    scale_ref[...] = over_fold(named_ref[...], folds, all_owners(chips))


def image_of(total, scale, binning, out_ref):
    tiles = out_ref.shape[0]
    total = total * jnp.concatenate([scale] * tiles, axis=0)
    image = bin_rows(total, binning, tiles)
    for g in range(tiles):
        out_ref[g] = image[:, g * PTS : (g + 1) * PTS].astype(out_ref.dtype)


def all_owners(chips):
    return [owner(chips, n, turn) for turn in range(2) for n in range(chips)]


def finish_kernel(chips, hi_ref, lo_ref, total_ref, named_ref, scale_ref, binning_ref, *refs):
    weights, out_ref = refs[:-1], refs[-1]
    owners = [owner(chips, n, turn) for turn in range(2) for n in range(1, chips)]
    total = total_ref[...] + weigh(hi_ref, lo_ref, named_ref[...], weights, owners, out_ref.shape[0])
    image_of(total, scale_ref[...], binning_ref[...], out_ref)


def own_kernel(chips, own_ref, near_ref, pattern_ref, spread_ref, code_ref, named_ref, scale_ref, binning_ref, *refs):
    weights, (out_ref, hi_ref, lo_ref) = refs[:-3], refs[-3:]
    tiles = out_ref.shape[0]
    chosen = choice(pattern_ref[...].astype(F32), spread_ref[...], code_ref[...])
    band_sums(chosen, own_ref, near_ref, hi_ref, lo_ref, tiles)
    total = weigh(hi_ref, lo_ref, named_ref[...], weights, all_owners(chips), tiles)
    image_of(total, scale_ref[...], binning_ref[...], out_ref)


def shards(traces, class_map, mid_bins, fold_count, weight_tiles, apertures):
    n_off = lax.axis_size("off")
    chips = n_off // 2
    tr_dev = traces.shape[0]
    tiles = apertures.shape[0]
    shape = jax.ShapeDtypeStruct

    def near(x):
        return lax.ppermute(x, "off", [(i, i ^ 1) for i in range(n_off)])

    def far(x, j, turn=0):
        return lax.ppermute(
            x, "off", [(i, (i // 2 + j) % chips * 2 + (i % 2 ^ turn)) for i in range(n_off)]
        )

    hops = range(1, chips)
    weights = weight_tiles.reshape(DEPTH, PTS)
    far_weights = [far(weights, j) for j in hops]
    block = shape((SUB, PTS), BF16)
    facts = call(facts_kernel, block, [pltpu.VMEM(block.shape, F32)], flops=FACTS_COST)(
        in_specs=[SMEM, VMEM], out_specs=VMEM
    )(fold_count, apertures)
    far_facts = [far(facts, j) for j in hops]
    tied, _ = lax.optimization_barrier((traces, facts))
    near_traces = near(tied)
    packet, again, *made = call(
        packet_kernel,
        (shape((DEPTH + SUB, PTS), BF16), block, shape((BANDS, BANDS * SUB), BF16),
         shape((NPAT * SUB, BANDS * SUB), F32)), [pltpu.VMEM(block.shape, F32)], flops=INFO_COST
    )(in_specs=[VMEM] * 4, out_specs=[VMEM] * 4)(
        facts, weights, mid_bins.reshape(1, tr_dev), class_map.reshape(1, tr_dev)
    )
    near_packet = near(packet)
    cross_facts = [far(again, j, 1) for j in hops]

    rows = 2 * tr_dev
    sums = shape((tiles * rows, NPAT * BAND), BF16)
    total = shape((tiles * rows, PTS), F32)
    by_row = shape((rows, PTS), F32)
    work = 2 * tiles * rows * (NPAT * BAND) * PTS
    relayed = [
        near(call(relay_kernel, shape(w.shape, BF16), flops=RELAY_COST)(
            in_specs=[ANY, VMEM, VMEM], out_specs=VMEM
        )(packet, traces, w))
        for w in far_weights
    ]
    known = [
        call(facts_in_kernel, block, flops=NEWS_COST)(in_specs=[VMEM] * 2, out_specs=VMEM)(traces, x)
        for x in far_facts
    ] + cross_facts
    all_begun = []
    for j in hops:
        begun, *its_sums, named, binning = call(
            functools.partial(begin_kernel, chips),
            (total, sums, sums, by_row, shape((MB, rows), BF16)),
        )(in_specs=[VMEM] * 7, out_specs=[VMEM] * 5)(
            traces, near_traces, known[j - 1], packet, near_packet, *made
        )
        all_begun.append((begun, *its_sums))
    scale = call(functools.partial(scale_kernel, chips), by_row, flops=SCALE_COST)(
        in_specs=[VMEM] * (3 + len(known)), out_specs=VMEM
    )(named, packet, near_packet, *known)
    received = []
    for j in hops:
        begun, *its_sums = all_begun[j - 1]
        rest = [begun, named, scale, binning] + far_weights + relayed
        part = call(functools.partial(finish_kernel, chips), shape((tiles, MB, PTS), BF16))(
            in_specs=[VMEM] * (2 + len(rest)), out_specs=VMEM
        )(*its_sums, *rest)
        received.append(far(part, chips - j))
    rest = [packet] + far_weights + [near_packet] + relayed
    image = call(
        functools.partial(own_kernel, chips), shape((tiles, MB, PTS), F32),
        [pltpu.VMEM(sums.shape, BF16)] * 2, flops=15 * work,
    )(in_specs=[VMEM] * (8 + len(rest)), out_specs=VMEM)(
        traces, near_traces, apertures, *made, named, scale, binning, *rest
    )
    for part in received:
        image = image + part.astype(F32)
    return image


def solution(mesh):
    placed = (
        P(("grp", "off", "tile"), None),
        P(("grp", "off", "tile"), None),
        P(("grp", "off", "tile")),
        P(("grp", "off")),
        P("off", None, None, None),
        P(("grp", "off", "tile"), None),
    )
    return jax.shard_map(
        shards,
        mesh=mesh,
        in_specs=placed,
        out_specs=P(("grp", "off", "tile"), None, None),
        check_vma=False,
    )
```

```python
import functools

import jax
import jax.numpy as jnp
from jax import lax
from jax.experimental import pallas as pl
from jax.experimental.pallas import tpu as pltpu
from jax.sharding import PartitionSpec as P

BANDS = 32
BAND = 128
PTS = 128
MB = 128
NPAT = 4
SUB = 16
DEPTH = NPAT * BAND
INFO_COST = 55 * 10**7
SCALE_COST = 8 * 10**8
FACTS_COST = 2 * 10**8
NEWS_COST = 6 * 10**9
RELAY_COST = 5 * 10**9
F32 = jnp.float32
BF16 = jnp.bfloat16
VMEM = pl.BlockSpec(memory_space=pltpu.VMEM)
ANY = pl.BlockSpec(memory_space=pl.ANY)
SMEM = pl.BlockSpec(memory_space=pltpu.SMEM)


def call(kernel, out, scratch=(), flops=0, moved=0, limit=24 << 20):
    return functools.partial(
        pl.pallas_call,
        kernel,
        out_shape=out,
        scratch_shapes=scratch,
        compiler_params=pltpu.CompilerParams(vmem_limit_bytes=limit),
        cost_estimate=pl.CostEstimate(flops=flops, bytes_accessed=moved, transcendentals=0),
    )


def facts_kernel(fold_ref, pattern_ref, facts_ref, facts):
    facts[...] = jnp.zeros_like(facts)
    facts[0:1] = jnp.full((1, PTS), fold_ref[0], jnp.int32).astype(F32)
    facts[8 : 8 + pattern_ref.shape[0], 0:BANDS] = pattern_ref[...].astype(F32)
    facts_ref[...] = facts[...].astype(BF16)


def packet_kernel(facts_ref, weight_ref, bins_ref, class_ref,
                  packet_ref, again_ref, spread_ref, code_ref, info):
    packet_ref[0:DEPTH] = weight_ref[...]
    info[...] = facts_ref[...].astype(F32)
    info[1:2] = bins_ref[...].astype(F32)
    info[2:3] = class_ref[...].astype(F32)
    packet_ref[DEPTH:] = info[...].astype(BF16)
    again_ref[...] = facts_ref[...]
    masks(spread_ref, code_ref)


def owner(chips, j, turn):
    me = lax.axis_index("off")
    core = lax.rem(me, 2)
    chip = lax.rem(me // 2 + chips - j, chips)
    return chip * 2 + (1 - core if turn else core)


def masks(spread_ref, code_ref):
    shape = spread_ref.shape
    band = lax.broadcasted_iota(jnp.int32, shape, 0)
    column = lax.broadcasted_iota(jnp.int32, shape, 1)
    spread_ref[...] = jnp.where(column // SUB == band, 1.0, 0.0).astype(BF16)
    row = lax.broadcasted_iota(jnp.int32, code_ref.shape, 0)
    col = lax.broadcasted_iota(jnp.int32, code_ref.shape, 1)
    code_ref[...] = jnp.where(row % SUB == col % SUB, (row // SUB + 1).astype(F32), -1.0)


def choice(pattern, spread, code):
    tiles = pattern.shape[0]
    padded = jnp.concatenate([pattern] * (8 // tiles), axis=0).astype(BF16)
    wide = jnp.dot(padded, spread, preferred_element_type=F32)
    return jnp.concatenate(
        [
            jnp.where(jnp.broadcast_to(wide[g : g + 1], code.shape) == code, 1.0, 0.0)
            for g in range(tiles)
        ],
        axis=0,
    ).astype(BF16)


def band_sums(chosen, own_ref, near_ref, hi_ref, lo_ref, tiles):
    traces = own_ref.shape[0]
    for half, ref in enumerate((own_ref, near_ref)):
        for pair in range(traces // (2 * SUB)):
            at = pair * 2 * SUB
            block = jnp.concatenate(
                [
                    jnp.concatenate(
                        [
                            ref[at + n * SUB : at + (n + 1) * SUB, b * BAND : (b + 1) * BAND]
                            for n in range(2)
                        ],
                        axis=1,
                    )
                    for b in range(BANDS)
                ],
                axis=0,
            )
            sums = jnp.dot(chosen, block, preferred_element_type=F32)
            for n in range(2):
                for g in range(tiles):
                    for a in range(NPAT):
                        top = (g * NPAT + a) * SUB
                        slab = sums[top : top + SUB, n * BAND : (n + 1) * BAND]
                        hi = slab.astype(BF16)
                        lo = (slab - hi.astype(F32)).astype(BF16)
                        to = (g * 2 + half) * traces + at + n * SUB
                        hi_ref[to : to + SUB, a * BAND : (a + 1) * BAND] = hi
                        lo_ref[to : to + SUB, a * BAND : (a + 1) * BAND] = lo


def weigh(hi_ref, lo_ref, named, weights, owners, tiles):
    total = None
    hi, lo = hi_ref[...], lo_ref[...]
    named = jnp.concatenate([named] * tiles, axis=0)
    for at in range(0, len(weights), 2):
        some = [w[0:DEPTH] for w in weights[at : at + 2]]
        wide = jnp.concatenate(some, axis=1) if len(some) > 1 else some[0]
        product = jnp.dot(hi, wide, preferred_element_type=F32) + jnp.dot(
            lo, wide, preferred_element_type=F32
        )
        for n in range(len(some)):
            mine = named == owners[at + n].astype(F32)
            part = jnp.where(mine, product[:, n * PTS : (n + 1) * PTS], 0.0)
            total = part if total is None else total + part
    return total


def over_fold(named, folds, owners):
    scale = jnp.zeros_like(named)
    for fold, held in zip(folds, owners):
        scale = jnp.where(named == held.astype(F32), 1.0 / fold, scale)
    return scale


def bin_rows(total, binning, tiles):
    rows = binning.shape[1]
    wide = jnp.concatenate([total[g * rows : (g + 1) * rows] for g in range(tiles)], axis=1)
    hi = wide.astype(BF16)
    lo = (wide - hi.astype(F32)).astype(BF16)
    return jnp.dot(binning, hi, preferred_element_type=F32) + jnp.dot(
        binning, lo, preferred_element_type=F32
    )


def facts_in_kernel(after_ref, facts_ref, out_ref):
    out_ref[...] = facts_ref[...]


def relay_kernel(after_ref, also_ref, weight_ref, out_ref):
    out_ref[...] = weight_ref[...]


def begin_kernel(chips, own_ref, near_ref, facts_ref, packet_ref, near_packet_ref, spread_ref, code_ref,
                 total_ref, hi_ref, lo_ref, named_ref, binning_ref):
    traces = own_ref.shape[0]
    tiles = hi_ref.shape[0] // (2 * traces)
    chosen = choice(facts_ref[...].astype(F32)[8 : 8 + tiles, 0:BANDS], spread_ref[...], code_ref[...])
    band_sums(chosen, own_ref, near_ref, hi_ref, lo_ref, tiles)
    for half, ref in enumerate((packet_ref, near_packet_ref)):
        at = half * traces
        info = ref[DEPTH:].astype(F32)
        place = lax.broadcasted_iota(jnp.int32, (MB, traces), 0).astype(F32)
        binning_ref[:, at : at + traces] = jnp.where(place == info[1:2], 1.0, 0.0).astype(BF16)
        named_ref[at : at + traces] = jnp.broadcast_to(info[2:3], (traces, traces)).T
    owners = [owner(chips, 0, 0), owner(chips, 0, 1)]
    weights = [packet_ref, near_packet_ref]
    total_ref[...] = weigh(hi_ref, lo_ref, named_ref[...], weights, owners, tiles)


def fold_scale(chips, named, packets, facts):
    folds = []
    for half, ref in enumerate(packets):
        folds.append(ref[DEPTH:].astype(F32)[0:1])
        for n in range(half * (chips - 1), (half + 1) * (chips - 1)):
            folds.append(facts[n][...].astype(F32)[0:1])
    return over_fold(named, folds, all_owners(chips))


def image_of(total, scale, binning, out_ref):
    tiles = out_ref.shape[0]
    total = total * jnp.concatenate([scale] * tiles, axis=0)
    image = bin_rows(total, binning, tiles)
    for g in range(tiles):
        out_ref[g] = image[:, g * PTS : (g + 1) * PTS].astype(out_ref.dtype)


def all_owners(chips):
    return [owner(chips, n, turn) for turn in range(2) for n in range(chips)]


def finish_kernel(chips, hi_ref, lo_ref, total_ref, named_ref, binning_ref, *refs):
    packets, refs, out_ref = refs[:2], refs[2:-1], refs[-1]
    facts, weights = refs[: 2 * (chips - 1)], refs[2 * (chips - 1) :]
    named = named_ref[...]
    owners = [owner(chips, n, turn) for turn in range(2) for n in range(1, chips)]
    scale = fold_scale(chips, named, packets, facts)
    total = total_ref[...] + weigh(hi_ref, lo_ref, named, weights, owners, out_ref.shape[0])
    image_of(total, scale, binning_ref[...], out_ref)


def own_kernel(chips, own_ref, near_ref, pattern_ref, spread_ref, code_ref, named_ref, binning_ref, *refs):
    facts, refs = refs[: 2 * (chips - 1)], refs[2 * (chips - 1) :]
    weights, (out_ref, hi_ref, lo_ref) = refs[:-3], refs[-3:]
    tiles = out_ref.shape[0]
    chosen = choice(pattern_ref[...].astype(F32), spread_ref[...], code_ref[...])
    band_sums(chosen, own_ref, near_ref, hi_ref, lo_ref, tiles)
    total = weigh(hi_ref, lo_ref, named_ref[...], weights, all_owners(chips), tiles)
    scale = fold_scale(chips, named_ref[...], (weights[0], weights[chips]), facts)
    image_of(total, scale, binning_ref[...], out_ref)


def shards(traces, class_map, mid_bins, fold_count, weight_tiles, apertures):
    n_off = lax.axis_size("off")
    chips = n_off // 2
    tr_dev = traces.shape[0]
    tiles = apertures.shape[0]
    shape = jax.ShapeDtypeStruct

    def near(x):
        return lax.ppermute(x, "off", [(i, i ^ 1) for i in range(n_off)])

    def far(x, j, turn=0):
        return lax.ppermute(
            x, "off", [(i, (i // 2 + j) % chips * 2 + (i % 2 ^ turn)) for i in range(n_off)]
        )

    hops = range(1, chips)
    weights = weight_tiles.reshape(DEPTH, PTS)
    far_weights = [far(weights, j) for j in hops]
    block = shape((SUB, PTS), BF16)
    facts = call(facts_kernel, block, [pltpu.VMEM(block.shape, F32)], flops=FACTS_COST)(
        in_specs=[SMEM, VMEM], out_specs=VMEM
    )(fold_count, apertures)
    far_facts = [far(facts, j) for j in hops]
    tied, _ = lax.optimization_barrier((traces, facts))
    near_traces = near(tied)
    packet, again, *made = call(
        packet_kernel,
        (shape((DEPTH + SUB, PTS), BF16), block, shape((BANDS, BANDS * SUB), BF16),
         shape((NPAT * SUB, BANDS * SUB), F32)), [pltpu.VMEM(block.shape, F32)], flops=INFO_COST
    )(in_specs=[VMEM] * 4, out_specs=[VMEM] * 4)(
        facts, weights, mid_bins.reshape(1, tr_dev), class_map.reshape(1, tr_dev)
    )
    near_packet = near(packet)
    cross_facts = [far(again, j, 1) for j in hops]

    rows = 2 * tr_dev
    sums = shape((tiles * rows, NPAT * BAND), BF16)
    total = shape((tiles * rows, PTS), F32)
    by_row = shape((rows, PTS), F32)
    work = 2 * tiles * rows * (NPAT * BAND) * PTS
    relayed = [
        near(call(relay_kernel, shape(w.shape, BF16), flops=RELAY_COST)(
            in_specs=[ANY, VMEM, VMEM], out_specs=VMEM
        )(packet, traces, w))
        for w in far_weights
    ]
    known = [
        call(facts_in_kernel, block, flops=NEWS_COST)(in_specs=[VMEM] * 2, out_specs=VMEM)(traces, x)
        for x in far_facts
    ]
    all_begun = []
    for j in hops:
        begun, *its_sums, named, binning = call(
            functools.partial(begin_kernel, chips),
            (total, sums, sums, by_row, shape((MB, rows), BF16)),
        )(in_specs=[VMEM] * 7, out_specs=[VMEM] * 5)(
            traces, near_traces, known[j - 1], packet, near_packet, *made
        )
        all_begun.append((begun, *its_sums))
    known += [
        call(facts_in_kernel, block, flops=SCALE_COST)(in_specs=[ANY, VMEM], out_specs=VMEM)(
            all_begun[0][0], x
        )
        for x in cross_facts
    ]
    received = []
    for j in hops:
        begun, *its_sums = all_begun[j - 1]
        rest = [begun, named, binning, packet, near_packet] + known + far_weights + relayed
        part = call(functools.partial(finish_kernel, chips), shape((tiles, MB, PTS), BF16))(
            in_specs=[VMEM] * (2 + len(rest)), out_specs=VMEM
        )(*its_sums, *rest)
        received.append(far(part, chips - j))
    rest = known + [packet] + far_weights + [near_packet] + relayed
    image = call(
        functools.partial(own_kernel, chips), shape((tiles, MB, PTS), F32),
        [pltpu.VMEM(sums.shape, BF16)] * 2, flops=15 * work,
    )(in_specs=[VMEM] * (7 + len(rest)), out_specs=VMEM)(
        traces, near_traces, apertures, *made, named, binning, *rest
    )
    for part in received:
        image = image + part.astype(F32)
    return image


def solution(mesh):
    placed = (
        P(("grp", "off", "tile"), None),
        P(("grp", "off", "tile"), None),
        P(("grp", "off", "tile")),
        P(("grp", "off")),
        P("off", None, None, None),
        P(("grp", "off", "tile"), None),
    )
    return jax.shard_map(
        shards,
        mesh=mesh,
        in_specs=placed,
        out_specs=P(("grp", "off", "tile"), None, None),
        check_vma=False,
    )
```
